32 devices in a mesh: sub: 4 (over z), crow: 4 (over x, core), ccol: 2 (over y).
Axes of the slice: x: 2, y: 2, z: 4, core: 2. Of those that a mesh axis runs over, the one named last changes fastest.
Arguments:
- load_cases: float32 [8, 1536, 256], P('sub', 'crow', 'ccol'), may hold values from -6 to 6
- stiffness: float32 [8, 1536, 1536], P('sub', 'crow'), may hold values from -1 to 6
- local_inverse: float32 [8, 1536, 1536], P('sub', 'crow'), may hold values from -1 to 1
- coarse_basis: float32 [8, 96, 1536], P('sub', None, 'crow'), may hold values from -0.15625 to 0.15625
- coarse_inverse: float32 [768, 768], P(('sub', 'crow')), may hold values from -1 to 3
- coupling: float32 [8, 6, 128, 128], P('sub'), may hold values from -0.5 to 0.5
- target_local_rows: int32 [8, 6, 128], P('sub'), may hold values from 0 to 1535
- neighbour_read_rows: int32 [8, 6, 128], P('sub'), may hold values from 0 to 1535
- neighbour: int32 [8, 6], P('sub'), may hold values from 0 to 7, as said below
- counts: int32 [8], P('sub'), may hold values from 1 to 6
Outputs:
- solution: float32 [8, 1536, 256], P('sub', 'crow', 'ccol')
- residual: float32 [8, 1536, 256], P('sub', 'crow', 'ccol')
The draws below stay inside these ranges and needn't reach their ends.
Inputs may be any that keep to these rules, and one draw needn't show every extreme that they name: neighbour[s, k] is a subdomain other than s, at most 2 away from s in the numbering. Only the first counts[s] interface blocks of subdomain s act. `target_local_rows`: rows may repeat within a block.
All inputs are finite; a program needn't handle non-finite values.
Results may differ from the reference program's by a relative error of at most 0.00013.
Values sent between devices are 32-bit elements; how exact they have to be, the bound alone decides.
No kernel may reach another device: no remote copies, remote signals or barrier semaphores. Data moves between devices by JAX's collectives and lax.ppermute only.
A program may use at most 64 MiB of HBM per device.

```python
import math
import jax
import jax.numpy as jnp
from jax import lax

LOCAL_UNKNOWNS = 1536
NEV = 96
INTERFACE_ROWS = 128
SLOT_COUNT = 6
NEIGHBOUR_REACH = 2
ITERS = 2
SUBDOMAIN_COUNT = 8
NC = 768
CASES = 256


def dominant(key, lead_shape, order_size, lower_end, upper_end, spread):
    key_diagonal, key_rest = jax.random.split(key)
    diagonal_part = jax.random.uniform(key_diagonal, lead_shape + (order_size,), jnp.float32, lower_end, upper_end)
    rest_reach = spread * math.sqrt(3.0 / order_size)
    rest_part = jax.random.uniform(key_rest, lead_shape + (order_size, order_size), jnp.float32, -rest_reach, rest_reach)
    return rest_part + diagonal_part[..., None] * jnp.eye(order_size, dtype=jnp.float32)


def draw_stiffness(key, part):
    return dominant(key, (SUBDOMAIN_COUNT,), LOCAL_UNKNOWNS, 2.0, 4.0, 1.0)


def draw_local_inverse(key, part):
    return dominant(key, (SUBDOMAIN_COUNT,), LOCAL_UNKNOWNS, 0.25, 0.5, 0.12)


def draw_coarse_inverse(key, part):
    return dominant(key, (), NC, 0.5, 1.5, 0.4)


def draw_neighbour(key, part):
    distance_key, side_key = jax.random.split(key)
    neighbour_distance = jax.random.randint(distance_key, (SUBDOMAIN_COUNT, SLOT_COUNT), 1, NEIGHBOUR_REACH + 1)
    sweep_direction = jax.random.randint(side_key, (SUBDOMAIN_COUNT, SLOT_COUNT), 0, 2) * 2 - 1
    own_index = jnp.arange(SUBDOMAIN_COUNT, dtype=jnp.int32)[:, None]
    candidate = own_index + neighbour_distance * sweep_direction
    outside = (candidate < 0) | (candidate >= SUBDOMAIN_COUNT)
    return jnp.where(outside, own_index - neighbour_distance * sweep_direction, candidate).astype(jnp.int32)


def place_ends(values, rng, low, top_value):
    shape = values.shape
    spot = [jax.random.randint(jax.random.fold_in(rng, axis), (), 0, shape[axis]) for axis in range(len(shape))]
    values = values.at[tuple(spot)].set(low)
    longest = shape.index(max(shape))
    spot[longest] = (spot[longest] + 1) % shape[longest]
    return values.at[tuple(spot)].set(top_value)


def levels(key, shape, cuts, low, high):
    factor_of = 1.0
    for position, blocks in cuts:
        steps = jax.random.uniform(jax.random.fold_in(jax.random.fold_in(key, 6), position), (blocks,), jnp.float32, low / len(cuts), high / len(cuts))
        factor_of = factor_of * jnp.repeat(jnp.exp(steps), shape[position] // blocks).reshape((-1,) + (1,) * (len(shape) - 1 - position))
    return factor_of


def normal_values(stream_key, shape, width, reach, pieces=(), held_as=jnp.bfloat16):
    drawn = jax.random.normal(stream_key, shape, jnp.float32) * width
    if len(pieces) > 0:
        drawn = levels(stream_key, shape, pieces, -0.22, 0.18) * drawn
    return jnp.clip(drawn, min=-reach, max=reach).astype(held_as)


def setup_inputs(seed: int = 0) -> dict:
    streams_of = jax.random.split(jax.random.key(seed), 11)
    load_cases = normal_values(streams_of[0], (SUBDOMAIN_COUNT, LOCAL_UNKNOWNS, CASES), 1.0, 6.0, ((0, 4), (1, 4), (2, 2)), jnp.float32)
    stiffness = draw_stiffness(jax.random.fold_in(streams_of[10], 71), 0)
    local_inverse = draw_local_inverse(jax.random.fold_in(streams_of[10], 71), 0)
    coarse_basis = normal_values(streams_of[3], (SUBDOMAIN_COUNT, NEV, LOCAL_UNKNOWNS), LOCAL_UNKNOWNS ** -0.5, 0.15625, ((0, 4), (2, 4)), jnp.float32)
    coarse_inverse = draw_coarse_inverse(jax.random.fold_in(streams_of[10], 71), 0)
    coupling = normal_values(streams_of[5], (SUBDOMAIN_COUNT, SLOT_COUNT, INTERFACE_ROWS, INTERFACE_ROWS), INTERFACE_ROWS ** -0.5, 0.5, ((0, 4),), jnp.float32)
    target_local_rows = place_ends(jax.random.randint(streams_of[6], (SUBDOMAIN_COUNT, SLOT_COUNT, INTERFACE_ROWS), 0, LOCAL_UNKNOWNS), jax.random.fold_in(streams_of[6], 1), 0, LOCAL_UNKNOWNS - 1).astype(jnp.int32)
    neighbour_read_rows = place_ends(jax.random.randint(streams_of[7], (SUBDOMAIN_COUNT, SLOT_COUNT, INTERFACE_ROWS), 0, LOCAL_UNKNOWNS), jax.random.fold_in(streams_of[7], 1), 0, LOCAL_UNKNOWNS - 1).astype(jnp.int32)
    neighbour = draw_neighbour(jax.random.fold_in(streams_of[10], 71), 0)
    counts = place_ends(jax.random.randint(streams_of[9], (SUBDOMAIN_COUNT,), 1, SLOT_COUNT + 1), jax.random.fold_in(streams_of[9], 1), 1, SLOT_COUNT).astype(jnp.int32)
    return dict(load_cases=load_cases, stiffness=stiffness, local_inverse=local_inverse, coarse_basis=coarse_basis, coarse_inverse=coarse_inverse, coupling=coupling, target_local_rows=target_local_rows, neighbour_read_rows=neighbour_read_rows, neighbour=neighbour, counts=counts)


damping = 0.7
highest_mode = lax.Precision.HIGHEST


def apply_operator(vector, stiffness, coupling, target_local_rows, neighbour_read_rows, neighbour, counts):
    local_part = jnp.einsum('slm,smc->slc', stiffness, vector, precision=highest_mode)
    sources = vector[neighbour[:, :, None], neighbour_read_rows]
    slot_terms = jnp.einsum('sknm,skmc->sknc', coupling, sources, precision=highest_mode)
    active_flag = (jnp.arange(SLOT_COUNT)[None, :] < counts[:, None]).astype(jnp.float32)
    slot_terms = slot_terms * active_flag[:, :, None, None]
    owners = jnp.broadcast_to(jnp.arange(SUBDOMAIN_COUNT)[:, None, None], target_local_rows.shape)
    inflow = jnp.zeros(vector.shape, jnp.float32).at[owners, target_local_rows].add(slot_terms)
    return local_part - inflow


def reference(load_cases, stiffness, local_inverse, coarse_basis, coarse_inverse, coupling, target_local_rows, neighbour_read_rows, neighbour, counts):
    solution = jnp.zeros_like(load_cases)
    residual = load_cases
    for sweep_index in range(ITERS):
        local_corr = jnp.einsum('slm,smc->slc', local_inverse, residual, precision=highest_mode)
        restricted = jnp.einsum('sel,slc->sec', coarse_basis, residual, precision=highest_mode)
        restricted = restricted.reshape(NC, CASES)
        coarse = jnp.dot(coarse_inverse, restricted, precision=highest_mode).reshape(SUBDOMAIN_COUNT, NEV, CASES)
        correction = local_corr + jnp.einsum('sel,sec->slc', coarse_basis, coarse, precision=highest_mode)
        solution = solution + damping * correction
        residual = residual - damping * apply_operator(correction, stiffness, coupling, target_local_rows, neighbour_read_rows, neighbour, counts)
    return solution, residual
```

```python
import jax
import jax.numpy as jnp
from jax import lax
from jax.experimental import pallas as pl
from jax.experimental.pallas import tpu as pltpu
from jax.sharding import PartitionSpec as P

ITERS = 2
damping = 0.7
f32 = jnp.float32
bf16 = jnp.bfloat16
MIB = 2**20
IN_VMEM = pl.BlockSpec(memory_space=pltpu.VMEM)
IN_SMEM = pl.BlockSpec(memory_space=pltpu.SMEM)


def call(kernel, name, operands, outputs, micros, scalars=0, scratch=(), limit=8):
    return pl.pallas_call(
        kernel,
        in_specs=[IN_SMEM] * scalars + [IN_VMEM] * (len(operands) - scalars),
        out_specs=[IN_VMEM] * len(outputs),
        out_shape=[jax.ShapeDtypeStruct(shape, kind) for shape, kind in outputs],
        scratch_shapes=list(scratch),
        compiler_params=pltpu.CompilerParams(vmem_limit_bytes=limit * MIB),
        cost_estimate=pl.CostEstimate(
            flops=0, bytes_accessed=int(micros * 3.6e6), transcendentals=0
        ),
        name=name,
    )(*operands)


def parts(x):
    hi = x.astype(bf16)
    return hi, (x - hi.astype(f32)).astype(bf16)


def beside(x):
    hi, lo = parts(x)
    return jnp.concatenate([hi, lo], axis=1)


def stacked(x):
    hi, lo = parts(x)
    return jnp.concatenate([hi, lo], axis=0)


def dot(a, b):
    return jnp.dot(a, b, preferred_element_type=f32)


def sides(product):
    columns = product.shape[1] // 2
    return product[:, :columns] + product[:, columns:]


def folded(product):
    rows = product.shape[0] // 2
    return sides(product[:rows] + product[rows:])


def exchange(x, axis, bit):
    size = lax.axis_size(axis)
    return lax.ppermute(x, axis, [(i, i ^ bit) for i in range(size) if (i ^ bit) < size])


def split_matrix(matrix, crow_index, name):
    subs, rows, order = matrix.shape

    def kernel(index, m, o):
        s, q = pl.program_id(0), pl.program_id(1)
        o[s, :, pl.ds(pl.multiple_of(q * rows, rows), rows)] = stacked(m[0])

    return pl.pallas_call(
        kernel,
        grid_spec=pltpu.PrefetchScalarGridSpec(
            num_scalar_prefetch=1,
            grid=(subs, order // rows),
            in_specs=[pl.BlockSpec((1, rows, rows), lambda s, q, index: (s, 0, index[0] ^ q))],
            out_specs=IN_VMEM,
        ),
        out_shape=jax.ShapeDtypeStruct((subs, 2 * rows, order), bf16),
        compiler_params=pltpu.CompilerParams(vmem_limit_bytes=8 * MIB),
        cost_estimate=pl.CostEstimate(
            flops=0, bytes_accessed=int(2.5 * 3.6e6), transcendentals=0
        ),
        name=name,
    )(crow_index.reshape(1), matrix)


def place_coarse(pieces, y_index, crow_index):
    basis_pieces = [p[0] for p in pieces]
    inverse_pieces = [p[1] for p in pieces]
    subs, modes, rows = basis_pieces[0].shape
    own_rows, columns = inverse_pieces[0].shape
    blocks = [p[2] for p in pieces]
    halves = [p[3] for p in pieces]
    count = max(blocks) + 1
    order = rows * count
    place = jnp.stack([y_index, crow_index])

    def kernel(at, *refs):
        basis_refs = refs[: len(pieces)]
        inverse_refs = refs[len(pieces) : 2 * len(pieces)]
        down, up, inverse = refs[2 * len(pieces) :]
        for b_ref, i_ref, q, half in zip(basis_refs, inverse_refs, blocks, halves):
            here = slice(q * rows, (q + 1) * rows)
            held = b_ref.shape[0]
            first = 0 if half is None else (at[0] if half == 0 else 1 - at[0]) * held
            for i in range(held):
                value = b_ref[i]
                down[first + i, :, here] = stacked(value)
                up[first + i, here] = beside(value.T)
            height = i_ref.shape[0]
            start = 0 if half is None else (at[0] if half == 0 else 1 - at[0]) * height
            inverse[at[1] ^ q, pl.ds(start, height)] = i_ref[...]

    return call(
        kernel,
        "place_coarse",
        [place] + basis_pieces + inverse_pieces,
        [
            ((subs, 2 * modes, order), bf16),
            ((subs, order, 2 * modes), bf16),
            ((count, own_rows, columns), f32),
        ],
        1.0,
        scalars=1,
    )


def split_targets(targets, order):
    subs, slots, width = targets.shape

    def kernel(tg, o):
        line = lax.broadcasted_iota(jnp.int32, (order, width), 0)
        for s in range(subs):
            for k in range(slots):
                hit = (line == tg[s, k : k + 1, :]).astype(f32).astype(bf16)
                o[s, :, k * width : (k + 1) * width] = hit

    return call(kernel, "split_targets", [targets], [((subs, order, slots * width), bf16)], 1.3)[0]


def own_part_restricted(basis, residual):
    subs, modes, rows = basis.shape
    cases = residual.shape[2]

    def kernel(z, r, o):
        for s in range(subs):
            o[s] = folded(dot(stacked(z[s]), beside(r[s])))

    return call(kernel, "own_part_restricted", [basis, residual], [((subs, modes, cases), f32)], 0.4)[0]


def load(ref, s):
    return ref[s] if len(ref.shape) == 3 else ref[...]


def local_solve(s, split, blocks):
    rows = split.shape[1] // 2
    order = split.shape[2]
    cases = blocks[0].shape[-1]

    def kernel(m, *refs):
        o, rhs = refs[-2:]
        for q, ref in enumerate(refs[:-2]):
            rhs[q * rows : (q + 1) * rows] = beside(load(ref, s))
        o[...] = folded(dot(m[s], rhs[...]))

    return call(
        kernel,
        "local_solve",
        [split, *blocks],
        [((rows, cases), f32)],
        0.8,
        scratch=[pltpu.VMEM((order, 2 * cases), bf16)],
    )[0]


def choose_terms(flag, mine, other, terms, width):
    slots = mine.shape[0]

    @pl.when(flag == 1)
    def _():
        for k in range(slots):
            terms[k * width : (k + 1) * width] = beside(mine[k])

    @pl.when(flag == 0)
    def _():
        for k in range(slots):
            terms[k * width : (k + 1) * width] = beside(other[k])


def local_solve_inflow(s, split, basis, blocks, hits, mine, other, flag):
    rows = split.shape[1] // 2
    order = split.shape[2]
    cases = blocks[0].shape[-1]
    modes = basis.shape[1] // 2
    slots, width = mine.shape[:2]
    count = len(blocks)

    def kernel(flag_ref, m, z, tg, g_mine, g_other, *refs):
        o, restricted, own, rhs, terms = refs[count:]
        choose_terms(flag_ref[s], g_mine, g_other, terms, width)
        for q, ref in enumerate(refs[:count]):
            here = slice(q * rows, (q + 1) * rows)
            r = ref[...] + damping * sides(dot(tg[s, here], terms[...]))
            if q == 0:
                own[...] = r
            rhs[here] = beside(r)
        restricted[...] = folded(dot(z[s], rhs[...]))
        o[...] = folded(dot(m[s], rhs[...]))

    return call(
        kernel,
        "local_solve_inflow",
        [flag, split, basis, hits, mine, other, *blocks],
        [((rows, cases), f32), ((modes, cases), f32), ((rows, cases), f32)],
        1.5,
        scalars=1,
        scratch=[
            pltpu.VMEM((order, 2 * cases), bf16),
            pltpu.VMEM((slots * width, 2 * cases), bf16),
        ],
    )


def correct(s, split, lift, inverse, place, mine, other, blocks, residual, old):
    rows = split.shape[1] // 2
    order = split.shape[2]
    cases = blocks[0].shape[-1]
    modes = lift.shape[2] // 2
    groups, half = mine.shape[:2]
    per_sub = inverse.shape[0] // split.shape[0]
    count = len(blocks)
    columns = inverse.shape[2]

    def kernel(at, m, z, c, g_mine, g_other, res, *refs):
        old_refs = refs[count : len(refs) - 4]
        o, total, corr, right = refs[len(refs) - 4 :]
        for b in range(groups):
            base = (at[0] ^ b) * (2 * half)
            right[pl.ds(pl.multiple_of(base + at[1] * half, half), half)] = beside(g_mine[b])
            right[pl.ds(pl.multiple_of(base + (1 - at[1]) * half, half), half)] = beside(g_other[b])
        c_rows = c[s * per_sub : (s + 1) * per_sub].reshape(modes, columns)
        coarse = beside(folded(dot(stacked(c_rows), right[...])))
        coarse = jnp.concatenate([coarse, coarse], axis=0)
        for q, ref in enumerate(refs[:count]):
            here = slice(q * rows, (q + 1) * rows)
            value = ref[...] + sides(dot(z[s, here], coarse))
            corr[here] = beside(value)
            if q == 0:
                total[...] = damping * value + old_refs[0][...] if old_refs else damping * value
        o[...] = load(res, s) - damping * folded(dot(m[s], corr[...]))

    return call(
        kernel,
        "correct",
        [place, split, lift, inverse, mine, other, residual, *blocks] + ([] if old is None else [old]),
        [((rows, cases), f32), ((rows, cases), f32), ((order, 2 * cases), bf16)],
        1.2,
        scalars=1,
        scratch=[pltpu.VMEM((columns, 2 * cases), bf16)],
        limit=12,
    )


def select_rows(where, lists, corrs):
    ways, slots, width = lists.shape
    order, twice = corrs[0].shape
    cases = twice // 2

    def kernel(where_ref, l, *refs):
        corr_refs = refs[: len(corrs)]
        outs = refs[len(corrs) :]
        lane = lax.broadcasted_iota(jnp.int32, (width, order), 1)
        for d in range(ways):

            @pl.loop(0, slots)
            def _(k):
                place = where_ref[d * slots + k]

                @pl.when(place < 0)
                def _():
                    outs[d][k] = jnp.zeros((width, cases), f32)

                for s, ref in enumerate(corr_refs):

                    @pl.when(place == s)
                    def _():
                        rows = jnp.broadcast_to(l[d, pl.ds(k, 1), :], (width, width)).T
                        rows = jnp.concatenate([rows] * (order // width), axis=1)
                        one = (rows == lane).astype(f32).astype(bf16)
                        outs[d][k] = sides(dot(one, ref[...]))

    return call(
        kernel,
        "select_rows",
        [where, lists, *corrs],
        [((slots, width, cases), f32)] * ways,
        1.5,
        scalars=1,
    )


def couple(codes, core, coupling, sources):
    slots, width = coupling.shape[1:3]
    cases = sources[0].shape[2]

    def kernel(codes_ref, core_ref, c, *refs):
        source_refs = refs[: len(sources)]
        out = refs[len(sources)]

        @pl.loop(0, slots)
        def _(k):
            code = codes_ref[k]

            @pl.when(code < 0)
            def _():
                out[k] = jnp.zeros((width, cases), f32)

            for d, ref in enumerate(source_refs):

                @pl.when(code == d)
                def _():
                    out[k] = folded(dot(stacked(c[core_ref[0], k]), beside(ref[k])))

    return call(
        kernel,
        "couple",
        [codes, core.reshape(1), coupling, *sources],
        [((slots, width, cases), f32)],
        0.8,
        scalars=2,
    )[0]


def add_inflow(residuals, hits, mine, other, flag):
    subs = hits.shape[0]
    slots, width = mine.shape[:2]
    rows, cases = residuals[0].shape

    def kernel(flag_ref, tg, g_mine, g_other, *refs):
        out, terms = refs[subs:]
        for s in range(subs):
            choose_terms(flag_ref[s], g_mine, g_other, terms, width)
            out[s] = refs[s][...] + damping * sides(dot(tg[s, :rows], terms[...]))

    return call(
        kernel,
        "add_inflow",
        [flag, hits, mine, other, *residuals],
        [((subs, rows, cases), f32)],
        0.8,
        scalars=1,
        scratch=[pltpu.VMEM((slots * width, 2 * cases), bf16)],
    )[0]


def coarse_pieces(basis, inverse, y_index):
    copies, size = lax.axis_size("ccol"), lax.axis_size("crow")
    pieces = [(basis, inverse, 0, None)]
    bit = size // 2
    while bit >= 1:
        news = []
        for z, c, q, half in pieces:
            if bit > 1 and copies == 2 and half is None:
                zh, ch = z.shape[0] // 2, c.shape[0] // 2
                z = exchange(lax.dynamic_slice_in_dim(z, y_index * zh, zh, 0), "crow", bit)
                c = exchange(lax.dynamic_slice_in_dim(c, y_index * ch, ch, 0), "crow", bit)
                news.append((z, c, q | bit, 0))
                news.append((exchange(z, "ccol", 1), exchange(c, "ccol", 1), q | bit, 1))
            else:
                news.append((exchange(z, "crow", bit), exchange(c, "crow", bit), q | bit, half))
        pieces = pieces + news
        bit //= 2
    return pieces


def gathered(x):
    bit = lax.axis_size("crow") // 2
    blocks = {0: x}
    while bit >= 1:
        blocks.update({q | bit: exchange(b, "crow", bit) for q, b in blocks.items()})
        bit //= 2
    return [blocks[q] for q in sorted(blocks)]


def spread_over_sub(half):
    half = half[None]
    bit = 1
    while bit < lax.axis_size("sub"):
        half = jnp.concatenate([half, exchange(half, "sub", bit)], axis=0)
        bit *= 2
    return half, exchange(half, "crow", 1)


def pair_routes(size):
    low = [(i, i + 1) for i in range(0, size - 1, 2)]
    high = [(i, i + 1) for i in range(1, size - 1, 2)]
    return [[p for a, b in pairs for p in ((a, b), (b, a))] for pairs in (low, high)]


def per_device(
    load_cases,
    stiffness,
    local_inverse,
    coarse_basis,
    coarse_inverse,
    coupling,
    target_local_rows,
    neighbour_read_rows,
    neighbour,
    counts,
):
    subs, rows, cases = load_cases.shape
    modes = coarse_basis.shape[1]
    slots = neighbour.shape[1]
    width = coupling.shape[3]
    groups = lax.axis_size("sub")
    crow_size = lax.axis_size("crow")
    group = lax.axis_index("sub")
    crow_index = lax.axis_index("crow")
    core = crow_index % 2
    y_index = lax.axis_index("ccol")
    half_subs = subs // 2

    first_blocks = gathered(load_cases)

    share = own_part_restricted(coarse_basis, load_cases)
    keep = lax.dynamic_slice_in_dim(share, core * half_subs, half_subs, 0)
    give = lax.dynamic_slice_in_dim(share, (1 - core) * half_subs, half_subs, 0)
    keep = (keep + exchange(give, "crow", 1)).reshape(half_subs * modes, cases)
    bit = 2
    while bit < crow_size:
        keep = keep + exchange(keep, "crow", bit)
        bit *= 2
    mine, other = spread_over_sub(keep)

    packed = jnp.concatenate(
        [
            neighbour_read_rows.reshape(subs * slots, width),
            jnp.pad(neighbour.reshape(1, subs * slots), ((0, 0), (0, width - subs * slots))),
            jnp.pad(counts.reshape(1, subs), ((0, 0), (0, width - subs))),
        ],
        axis=0,
    )
    routes = pair_routes(groups)
    all_lists = [packed] + [lax.ppermute(packed, "sub", route) for route in routes]
    slot = jnp.arange(slots, dtype=jnp.int32)
    wheres, lists = [], []
    for held in all_lists:
        reads = lax.dynamic_slice_in_dim(
            held[: subs * slots].reshape(subs, slots, width), core * half_subs, half_subs, 0
        ).reshape(half_subs * slots, width)
        ids = held[subs * slots, : subs * slots].reshape(subs, slots)
        limits = held[subs * slots + 1, :subs]
        place = ids - group * subs
        use = (slot[None, :] < limits[:, None]) & (place >= 0) & (place < subs)
        place = lax.dynamic_slice_in_dim(jnp.where(use, place, -1), core * half_subs, half_subs, 0)
        wheres.append(place.reshape(-1))
        lists.append(((reads // rows) ^ crow_index) * rows + reads % rows)
    where = jnp.concatenate(wheres)
    lists = jnp.stack(lists)
    source_group = neighbour // subs
    code = jnp.where(source_group == group, 0, jnp.where(source_group == (group ^ 1), 1, 2))
    active = slot[None, :] < counts[:, None]
    code = jnp.where(active, code, -1)
    codes = lax.dynamic_slice_in_dim(code, core * half_subs, half_subs, 0).reshape(-1)
    targets = ((target_local_rows // rows) ^ crow_index) * rows + target_local_rows % rows
    hits = split_targets(jnp.where(active[:, :, None], targets, -1), crow_size * rows)
    flag = (jnp.arange(subs, dtype=jnp.int32) // half_subs == core).astype(jnp.int32)
    place = jnp.stack([group, core])

    inverse_split = split_matrix(local_inverse, crow_index, "split_inverse")
    stiffness_split = split_matrix(stiffness, crow_index, "split_stiffness")
    down, lift, inverse = place_coarse(
        coarse_pieces(coarse_basis, coarse_inverse, y_index), y_index, crow_index
    )

    totals, residuals = [None] * subs, [load_cases] * subs
    local = [local_solve(s, inverse_split, first_blocks) for s in range(subs)]
    for sweep_index in range(ITERS):
        local_blocks = [gathered(v) for v in local]
        steps = [
            correct(
                s, stiffness_split, lift, inverse, place, mine, other,
                local_blocks[s], residuals[s], totals[s],
            )
            for s in range(subs)
        ]
        passed, totals, corrs = zip(*steps)
        chosen = select_rows(where, lists, corrs)
        sources = [chosen[0]] + [lax.ppermute(c, "sub", route) for c, route in zip(chosen[1:], routes)]
        terms = couple(codes, core, coupling, sources)
        other_terms = exchange(terms, "crow", 1)
        if sweep_index == ITERS - 1:
            return jnp.stack(totals), add_inflow(passed, hits, terms, other_terms, flag)
        steps = [
            local_solve_inflow(
                s, inverse_split, down, gathered(passed[s]), hits, terms, other_terms, flag
            )
            for s in range(subs)
        ]
        local, restricted, residuals = zip(*steps)
        keep = lax.dynamic_slice_in_dim(jnp.stack(restricted), core * half_subs, half_subs, 0)
        mine, other = spread_over_sub(keep.reshape(half_subs * modes, cases))


def solution(mesh):
    return jax.shard_map(
        per_device,
        mesh=mesh,
        in_specs=(
            P("sub", "crow", "ccol"),
            P("sub", "crow", None),
            P("sub", "crow", None),
            P("sub", None, "crow"),
            P(("sub", "crow"), None),
            P("sub", None, None, None),
            P("sub", None, None),
            P("sub", None, None),
            P("sub", None),
            P("sub"),
        ),
        out_specs=(P("sub", "crow", "ccol"), P("sub", "crow", "ccol")),
        check_vma=False,
    )
```

```python
import jax
import jax.numpy as jnp
from jax import lax
from jax.experimental import pallas as pl
from jax.experimental.pallas import tpu as pltpu
from jax.sharding import PartitionSpec as P

ITERS = 2
damping = 0.7
f32 = jnp.float32
bf16 = jnp.bfloat16
MIB = 2**20
COST = 1000.0
IN_VMEM = pl.BlockSpec(memory_space=pltpu.VMEM)
IN_SMEM = pl.BlockSpec(memory_space=pltpu.SMEM)
IN_HBM = pl.BlockSpec(memory_space=pltpu.HBM)


def call(kernel, name, operands, outputs, micros, scalars=0, scratch=(), limit=8, far=0, after=()):
    used = len(operands)

    def body(*refs):
        kernel(*refs[:used], *refs[used + len(after) :])

    operands = list(operands[: used - far]) + [
        pltpu.with_memory_space_constraint(x, pltpu.HBM) for x in operands[used - far :]
    ]
    return pl.pallas_call(
        body,
        in_specs=[IN_SMEM] * scalars
        + [IN_VMEM] * (used - scalars - far)
        + [IN_HBM] * far
        + [pl.BlockSpec(memory_space=pl.ANY)] * len(after),
        out_specs=[IN_SMEM if len(shape) == 1 else IN_VMEM for shape, _ in outputs],
        out_shape=[jax.ShapeDtypeStruct(shape, kind) for shape, kind in outputs],
        scratch_shapes=list(scratch),
        compiler_params=pltpu.CompilerParams(vmem_limit_bytes=limit * MIB),
        cost_estimate=pl.CostEstimate(flops=0, bytes_accessed=int(micros * COST), transcendentals=0),
        name=name,
    )(*operands, *after)


def position():
    crow = lax.axis_index("crow")
    return lax.axis_index("sub"), lax.rem(crow, 2), crow


def parts(x):
    hi = x.astype(bf16)
    return hi, (x - hi.astype(f32)).astype(bf16)


def beside(x):
    hi, lo = parts(x)
    return jnp.concatenate([hi, lo], axis=1)


def stacked(x):
    hi, lo = parts(x)
    return jnp.concatenate([hi, lo], axis=0)


def dot(a, b):
    return jnp.dot(a, b, preferred_element_type=f32)


def sides(product):
    columns = product.shape[1] // 2
    return product[:, :columns] + product[:, columns:]


def folded(product):
    rows = product.shape[0] // 2
    return sides(product[:rows] + product[rows:])


def exchange(x, axis, bit):
    size = lax.axis_size(axis)
    return lax.ppermute(x, axis, [(i, i ^ bit) for i in range(size) if (i ^ bit) < size])


def split_matrix(matrix, name, after=()):
    subs, rows, order = matrix.shape
    tile = 96 if rows % 96 == 0 else rows
    tiles = rows // tile

    def kernel(m, o, held, sems):
        crow = lax.axis_index("crow")
        copies = [
            pltpu.make_async_copy(
                m.at[i // tiles, pl.ds((i % tiles) * tile, tile)], held.at[i], sems.at[i]
            )
            for i in range(subs * tiles)
        ]
        for copy in copies:
            copy.start()
        for i, copy in enumerate(copies):
            copy.wait()
            first = (i % tiles) * tile
            for q in range(order // rows):
                column = pl.multiple_of((crow ^ q) * rows, 128)
                hi, lo = parts(held[i, :, pl.ds(column, rows)])
                o[i // tiles, first : first + tile, q * rows : (q + 1) * rows] = hi
                o[i // tiles, rows + first : rows + first + tile, q * rows : (q + 1) * rows] = lo

    return call(
        kernel,
        name,
        [matrix],
        [((subs, 2 * rows, order), bf16)],
        2.0,
        far=1,
        scratch=[
            pltpu.VMEM((subs * tiles, tile, order), f32),
            pltpu.SemaphoreType.DMA((subs * tiles,)),
        ],
        after=after,
    )[0]


def place_coarse(pieces, subs, modes, own_rows, after=()):
    height, rows = pieces[0][0].shape
    count = max(q for _, q, _ in pieces) + 1
    order = rows * count
    spans = (height - subs * modes) // own_rows

    def kernel(*refs):
        down, up, inverse, held = refs[len(pieces) :]
        crow, ccol = lax.axis_index("crow"), lax.axis_index("ccol")
        for ref, (_, q, half) in zip(refs, pieces):
            if half is None:
                held[q] = ref[...]
            else:
                size = ref.shape[0]
                which = ccol if half == 0 else 1 - ccol
                held[q, pl.ds(pl.multiple_of(which * size, 8), size)] = ref[...]
        for q in range(count):
            here = slice(q * rows, (q + 1) * rows)
            for s in range(subs):
                value = held[q, s * modes : (s + 1) * modes]
                down[s, :, here] = stacked(value)
                up[s, here] = beside(value.T)
            for i in range(spans):
                first = subs * modes + i * own_rows
                inverse[crow ^ q, :, i * rows : (i + 1) * rows] = held[q, first : first + own_rows]

    return call(
        kernel,
        "place_coarse",
        [p[0] for p in pieces],
        [
            ((subs, 2 * modes, order), bf16),
            ((subs, order, 2 * modes), bf16),
            ((count, own_rows, spans * rows), f32),
        ],
        1.2,
        scratch=[pltpu.VMEM((count, height, rows), f32)],
        limit=16,
        after=after,
    )


def fold_targets(counts, targets, split, basis, after=()):
    slots, subs, width = targets.shape
    rows = split.shape[1] // 2
    order = split.shape[2]
    modes = basis.shape[1] // 2
    half = subs // 2

    def kernel(n, tg, m, z, own, folds, z_folds):
        at = position()
        line = lax.broadcasted_iota(jnp.int32, (order, width), 0)
        for s in range(subs):
            for k in range(0, slots, 2):
                pair = []
                for kk in (k, k + 1):
                    aim = in_xor_order(tg[kk, s : s + 1, :], rows, order // rows, at[2])
                    aim = jnp.where(kk < n[s], aim, -1)
                    pair.append((line == aim).astype(f32).astype(bf16))
                hit = jnp.concatenate(pair, axis=1)
                here = slice(k * width, (k + 2) * width)
                own[s, :, here] = hit[:rows]
                folds[s, :, here] = dot(m[s], hit).astype(bf16)

                @pl.when(at[1] == s // half)
                def _():
                    z_folds[s % half, :, here] = dot(z[s], hit).astype(bf16)

    return call(
        kernel,
        "fold_targets",
        [counts, targets, split, basis],
        [
            ((subs, rows, slots * width), bf16),
            ((subs, 2 * rows, slots * width), bf16),
            ((half, 2 * modes, slots * width), bf16),
        ],
        4.5,
        scalars=1,
        limit=8,
        after=after,
    )


def begin(neighbour, counts, reads, basis, residual, inverse):
    subs, modes, rows = basis.shape
    cases = residual.shape[2]
    half = subs // 2
    slots, _, width = reads.shape
    used = subs * slots
    listed = -(-(used + 2) // 8) * 8
    own_rows, columns = inverse.shape
    height = subs * modes + own_rows * (columns // rows)

    def kernel(n, c, rd, z_far, r_far, c_far, keep, give, r, packed, both, part, sems):
        at = position()
        pairs = [(z_far.at[s], both.at[s * modes : (s + 1) * modes]) for s in range(subs)]
        pairs.append((r_far, r))
        for i in range(columns // rows):
            first = subs * modes + i * own_rows
            pairs.append((c_far.at[:, i * rows : (i + 1) * rows], both.at[first : first + own_rows]))
        moves = [pltpu.make_async_copy(a, b, sems.at[i]) for i, (a, b) in enumerate(pairs)]
        for move in moves:
            move.start()
        lane = lax.broadcasted_iota(jnp.int32, (1, width), 1)
        ids = jnp.zeros((1, width), jnp.int32)
        limits = jnp.zeros((1, width), jnp.int32)
        packed[...] = jnp.zeros((listed, width), f32)
        for s in range(subs):
            for k in range(slots):
                block = s * slots + k
                packed[block : block + 1] = rd[k, s : s + 1].astype(f32)
                ids = jnp.where(lane == block, n[s, k], ids)
                limits = jnp.where(lane == block, jnp.where(k < c[s], 1, 0), limits)
        packed[used : used + 1] = ids.astype(f32)
        packed[used + 1 : used + 2] = limits.astype(f32)
        for move in moves:
            move.wait()
        start = pl.multiple_of(lax.axis_index("ccol") * (height // 2), 8)
        part[...] = both[pl.ds(start, height // 2)]
        for i in range(half):
            for out, first in ((keep, at[1] * half), (give, (1 - at[1]) * half)):
                s = first + i
                z = both[pl.ds(pl.multiple_of(s * modes, modes), modes)]
                out[i * modes : (i + 1) * modes] = folded(dot(stacked(z), beside(r[s])))

    return call(
        kernel,
        "begin",
        [neighbour, counts, reads, basis, residual, inverse],
        [
            ((half * modes, cases), f32),
            ((half * modes, cases), f32),
            (residual.shape, f32),
            ((listed, width), f32),
            ((height, rows), f32),
            ((height // 2, rows), f32),
        ],
        2.0,
        scalars=2,
        far=3,
        scratch=[pltpu.SemaphoreType.DMA((subs + 1 + columns // rows,))],
    )


def relay(x, after):
    def kernel(a, b):
        b[...] = a[...]

    return call(kernel, "relay", [x], [(x.shape, x.dtype)], 0.3, after=after)[0]


def in_xor_order(rows_listed, rows, blocks, crow_index):
    block = jnp.zeros_like(rows_listed)
    for q in range(1, blocks):
        block = block + (rows_listed >= q * rows).astype(jnp.int32)
    return rows_listed + ((block ^ crow_index) - block) * rows


def prepare(held, subs, slots, rows, blocks, after=()):
    ways = len(held)
    width = held[0].shape[1]
    used = subs * slots
    half = used // 2
    listed = -(-(used + 2) // 8) * 8
    starts = [h.shape[0] - listed for h in held]

    def kernel(*refs):
        at = position()
        lists, info, rows_v, sem = refs[ways:]
        for d in range(ways):
            table = refs[d][starts[d] : starts[d] + listed].astype(jnp.int32)
            picked = jnp.where(at[1] == 0, table[:half], table[half:used])
            lists[d] = in_xor_order(picked, rows, blocks, at[2])
            ids, limits = table[used : used + 1], table[used + 1 : used + 2]
            place = ids - at[0] * subs
            use = (limits > 0) & (place >= 0) & (place < subs)
            rows_v[d : d + 1] = jnp.where(use, place, -1)
        table = refs[0][starts[0] : starts[0] + listed].astype(jnp.int32)
        ids, limits = table[used : used + 1], table[used + 1 : used + 2]
        twin = at[0] ^ 1
        inside = (ids >= at[0] * subs) & (ids < (at[0] + 1) * subs)
        paired = (ids >= twin * subs) & (ids < (twin + 1) * subs)
        theirs = jnp.where(inside, 0, jnp.where(paired, 1, 2))
        rows_v[ways : ways + 1] = jnp.where(limits > 0, theirs, -1)
        move = pltpu.make_async_copy(rows_v, info, sem)
        move.start()
        move.wait()

    return pl.pallas_call(
        lambda *refs: kernel(*refs[:ways], *refs[ways + len(after) :]),
        in_specs=[IN_VMEM] * ways + [pl.BlockSpec(memory_space=pl.ANY)] * len(after),
        out_specs=[IN_VMEM, IN_SMEM],
        out_shape=[
            jax.ShapeDtypeStruct((ways, half, width), jnp.int32),
            jax.ShapeDtypeStruct((8, width), jnp.int32),
        ],
        scratch_shapes=[pltpu.VMEM((8, width), jnp.int32), pltpu.SemaphoreType.DMA(())],
        compiler_params=pltpu.CompilerParams(vmem_limit_bytes=8 * MIB),
        cost_estimate=pl.CostEstimate(flops=0, bytes_accessed=int(COST), transcendentals=0),
        name="prepare",
    )(*held, *after)


def add_up(a, b, below=None, after=()):
    rows = a.shape[0]
    more = 0 if below is None else below.shape[0]

    def kernel(x, y, *refs):
        o = refs[-1]
        o[:rows] = x[...] + y[...]
        if more:
            o[rows:] = refs[0][...]

    operands = [a, b] + ([] if below is None else [below])
    return call(kernel, "add_up", operands, [((rows + more, a.shape[1]), f32)], 0.2, after=after)[0]


def load(ref, s):
    return ref[s] if len(ref.shape) == 3 else ref[...]


def local_solve(s, split, blocks, after=()):
    rows = split.shape[1] // 2
    order = split.shape[2]
    cases = blocks[0].shape[-1]

    def kernel(m, *refs):
        o, rhs = refs[-2:]
        for q, ref in enumerate(refs[:-2]):
            rhs[q * rows : (q + 1) * rows] = beside(load(ref, s))
        o[...] = folded(dot(m[s], rhs[...]))

    return call(
        kernel,
        "local_solve",
        [split, *blocks],
        [((rows, cases), f32)],
        0.8,
        scratch=[pltpu.VMEM((order, 2 * cases), bf16)],
        after=after,
    )[0]


def choose_terms(here, mine, other, terms):
    slots, width = mine.shape[:2]

    @pl.when(here)
    def _():
        for k in range(slots):
            terms[k * width : (k + 1) * width] = beside(mine[k])

    @pl.when(jnp.logical_not(here))
    def _():
        for k in range(slots):
            terms[k * width : (k + 1) * width] = beside(other[k])


def local_solve_inflow(s, split, folds, blocks, mine, other, after=()):
    rows = split.shape[1] // 2
    order = split.shape[2]
    subs = split.shape[0]
    cases = blocks[0].shape[-1]
    slots, width = mine.shape[:2]
    count = len(blocks)

    def kernel(m, f, g_mine, g_other, *refs):
        at = position()
        o, rhs, terms = refs[count:]
        for q, ref in enumerate(refs[:count]):
            rhs[q * rows : (q + 1) * rows] = beside(ref[...])
        choose_terms(at[1] == s // (subs // 2), g_mine, g_other, terms)
        o[...] = folded(dot(m[s], rhs[...])) + damping * folded(dot(f[s], terms[...]))

    return call(
        kernel,
        "local_solve_inflow",
        [split, folds, mine, other, *blocks],
        [((rows, cases), f32), ((order, 2 * cases), bf16)],
        1.2,
        scratch=[pltpu.VMEM((slots * width, 2 * cases), bf16)],
        after=after,
    )


def restrict(basis, z_folds, residual_parts, terms, after=()):
    subs = basis.shape[0]
    modes = basis.shape[1] // 2
    cases = residual_parts[0].shape[1] // 2
    half = subs // 2
    slots, width = terms.shape[0] // half, terms.shape[1]

    def kernel(z, zf, g, *refs):
        at = position()
        out, rhs = refs[subs:]
        for i in range(half):
            for k in range(slots):
                rhs[k * width : (k + 1) * width] = beside(g[i * slots + k])
            inflow = damping * folded(dot(zf[i], rhs[...]))
            for s in range(i, subs, half):

                @pl.when(at[1] == s // half)
                def _():
                    out[i * modes : (i + 1) * modes] = folded(dot(z[s], refs[s][...])) + inflow

    return call(
        kernel,
        "restrict",
        [basis, z_folds, terms, *residual_parts],
        [((half * modes, cases), f32)],
        0.4,
        scratch=[pltpu.VMEM((slots * width, 2 * cases), bf16)],
        after=after,
    )[0]


def lift_coarse(inverse, lift, mine, other, after=()):
    subs, order, twice = lift.shape
    modes = twice // 2
    half, cases = subs // 2, mine[0].shape[1]
    per_sub = inverse.shape[0] // subs
    columns = inverse.shape[2]
    groups = len(mine)

    def kernel(c, z, *refs):
        at = position()
        o, right = refs[2 * groups :]
        for b in range(groups):
            base = (at[0] ^ b) * (2 * half * modes)
            for h, ref in ((at[1], refs[b]), (1 - at[1], refs[groups + b])):
                for i in range(half):
                    row = pl.multiple_of(base + h * (half * modes) + i * modes, 16)
                    right[pl.ds(row, modes)] = beside(ref[i * modes : (i + 1) * modes])
        for s in range(subs):
            c_rows = c[s * per_sub : (s + 1) * per_sub].reshape(modes, columns)
            coarse = beside(folded(dot(stacked(c_rows), right[...])))
            o[s] = sides(dot(z[s], jnp.concatenate([coarse, coarse], axis=0)))

    return call(
        kernel,
        "lift_coarse",
        [inverse, lift, *mine, *other],
        [((subs, order, cases), f32)],
        1.2,
        scratch=[pltpu.VMEM((columns, 2 * cases), bf16)],
        limit=16,
        after=after,
    )[0]


def correct(s, split, lifted, blocks, residual, old, after=()):
    rows = split.shape[1] // 2
    order = split.shape[2]
    cases = blocks[0].shape[-1]
    count = len(blocks)

    def kernel(m, up, res, *refs):
        old_refs = refs[count : len(refs) - 3]
        o, total, corr = refs[len(refs) - 3 :]
        for q, ref in enumerate(refs[:count]):
            here = slice(q * rows, (q + 1) * rows)
            value = ref[...] + up[s, here]
            corr[here] = beside(value)
            if q == 0:
                total[...] = damping * value + old_refs[0][...] if old_refs else damping * value
        o[...] = load(res, s) - damping * folded(dot(m[s], corr[...]))

    return call(
        kernel,
        "correct",
        [split, lifted, residual, *blocks] + ([] if old is None else [old]),
        [((rows, cases), f32), ((rows, cases), f32), ((order, 2 * cases), bf16)],
        1.0,
        after=after,
    )


def select_rows(info, lists, corrs, after=()):
    ways, slots, width = lists.shape
    order, twice = corrs[0].shape
    cases = twice // 2

    def kernel(where, l, *refs):
        at = position()
        corr_refs = refs[: len(corrs)]
        outs = refs[len(corrs) :]
        lane = lax.broadcasted_iota(jnp.int32, (width, order), 1)
        for d in range(ways):

            @pl.loop(0, slots)
            def _(k):
                place = where[d, at[1] * slots + k]

                @pl.when(place < 0)
                def _():
                    outs[d][k] = jnp.zeros((width, cases), f32)

                for s, ref in enumerate(corr_refs):

                    @pl.when(place == s)
                    def _():
                        rows = jnp.broadcast_to(l[d, pl.ds(k, 1), :], (width, width)).T
                        rows = jnp.concatenate([rows] * (order // width), axis=1)
                        one = (rows == lane).astype(f32).astype(bf16)
                        outs[d][k] = sides(dot(one, ref[...]))

    return call(
        kernel,
        "select_rows",
        [info, lists, *corrs],
        [((slots, width, cases), f32)] * ways,
        1.5,
        scalars=1,
        after=after,
    )


def couple(info, coupling, sources, after=()):
    subs, per_sub, width, _ = coupling.shape
    slots, _, cases = sources[0].shape
    ways = len(sources)

    def kernel(where, c, *refs):
        at = position()
        out = refs[ways]

        @pl.loop(0, slots)
        def _(k):
            block = at[1] * slots + k
            code = where[ways, block]

            @pl.when(code < 0)
            def _():
                out[k] = jnp.zeros((width, cases), f32)

            for d, ref in enumerate(refs[:ways]):

                @pl.when(code == d)
                def _():
                    out[k] = folded(dot(stacked(c[block // per_sub, block % per_sub]), beside(ref[k])))

    return call(
        kernel,
        "couple",
        [info, coupling, *sources],
        [((slots, width, cases), f32)],
        0.8,
        scalars=1,
        after=after,
    )[0]


def add_inflow(residuals, hits, mine, other):
    subs = hits.shape[0]
    slots, width, cases = mine[0].shape
    rows = residuals[0].shape[0]
    sweeps = len(mine)

    def kernel(tg, *refs):
        at = position()
        groups = (refs[:sweeps], refs[sweeps : 2 * sweeps])
        res = refs[2 * sweeps : 2 * sweeps + subs]
        out, terms = refs[2 * sweeps + subs :]
        for s in range(subs):
            here = at[1] == s // (subs // 2)
            for flag, terms_of in ((here, groups[0]), (jnp.logical_not(here), groups[1])):

                @pl.when(flag)
                def _():
                    for k in range(slots):
                        value = terms_of[0][k]
                        for more in terms_of[1:]:
                            value = value + more[k]
                        terms[k * width : (k + 1) * width] = beside(value)

            out[s] = res[s][...] + damping * sides(dot(tg[s], terms[...]))

    return call(
        kernel,
        "add_inflow",
        [hits, *mine, *other, *residuals],
        [((subs, rows, cases), f32)],
        0.8,
        scratch=[pltpu.VMEM((slots * width, 2 * cases), bf16)],
    )[0]


def gathered(x, hold=()):
    bit = lax.axis_size("crow") // 2
    blocks = {0: x}
    while bit >= 1:
        news = {q | bit: exchange(b, "crow", bit) for q, b in blocks.items()}
        if bit > 1 and hold:
            news = {q: relay(b, hold) for q, b in news.items()}
        blocks.update(news)
        bit //= 2
    return [blocks[q] for q in sorted(blocks)]


def coarse_pieces(x, part, hold):
    bit = lax.axis_size("crow") // 2
    if lax.axis_size("ccol") == 2:
        part = relay(exchange(part, "crow", bit), hold)
        pieces = [(x, 0, None), (part, bit, 0), (exchange(part, "ccol", 1), bit, 1)]
    else:
        pieces = [(x, 0, None), (exchange(x, "crow", bit), bit, None)]
    while bit > 1:
        bit //= 2
        pieces = pieces + [(exchange(p, "crow", bit), q | bit, half) for p, q, half in pieces]
    return pieces


def spread_over_sub(half):
    halves = [half] + [exchange(half, "sub", b) for b in range(1, lax.axis_size("sub"))]
    return halves, [exchange(h, "crow", 1) for h in halves]


def pair_routes(size):
    low = [(i, i + 1) for i in range(0, size - 1, 2)]
    high = [(i, i + 1) for i in range(1, size - 1, 2)]
    return [[p for a, b in pairs for p in ((a, b), (b, a))] for pairs in (low, high)]


def per_device(
    load_cases,
    stiffness,
    local_inverse,
    coarse_basis,
    coarse_inverse,
    coupling,
    target_local_rows,
    neighbour_read_rows,
    neighbour,
    counts,
):
    subs, rows, cases = load_cases.shape
    slots = neighbour.shape[1]
    groups = lax.axis_size("sub")
    crow_size = lax.axis_size("crow")
    targets = target_local_rows.transpose(1, 0, 2)
    routes = pair_routes(groups)

    keep, give, residual, packed, both, part = begin(
        neighbour, counts, neighbour_read_rows.transpose(1, 0, 2), coarse_basis, load_cases,
        coarse_inverse,
    )
    keep = add_up(keep, exchange(give, "crow", 1), None, [keep])
    inverse_split = split_matrix(local_inverse, "split_inverse", [keep])
    first_blocks = gathered(load_cases, [inverse_split])
    bits = [bit for bit in (2, 4, 8) if bit < crow_size]
    for bit in bits[:-1]:
        keep = add_up(keep, exchange(keep, "crow", bit), None, [inverse_split])
    more = relay(exchange(keep, "crow", bits[-1]), [inverse_split])
    local = []
    for s in range(subs):
        local.append(local_solve(s, inverse_split, first_blocks, [more] if s == 0 else [local[-1]]))
    keep = add_up(keep, more, packed, [local[-1]])
    mine, other = spread_over_sub(keep)

    if groups == 4:
        held = [packed, mine[1], mine[3]]
    else:
        held = [packed] + [lax.ppermute(packed, "sub", route) for route in routes]

    down, lift, inverse = place_coarse(
        coarse_pieces(both, part, [keep]), subs, coarse_basis.shape[1], coarse_inverse.shape[0],
        [keep],
    )
    lists, info = prepare(held, subs, slots, rows, crow_size, [down])
    stiffness_split = split_matrix(stiffness, "split_stiffness", [info])

    totals, residuals, last = [None] * subs, [residual] * subs, stiffness_split
    all_terms, all_others = [], []
    for sweep_index in range(ITERS):
        local_blocks = [gathered(v) for v in local]
        lifted = lift_coarse(inverse, lift, mine, other, [last])
        steps, last = [], lifted
        for s in range(subs):
            steps.append(
                correct(s, stiffness_split, lifted, local_blocks[s], residuals[s], totals[s], [last])
            )
            last = steps[-1][0]
        residuals, totals, corrs = zip(*steps)
        chosen = select_rows(info, lists, corrs)
        sources = [chosen[0]] + [lax.ppermute(c, "sub", route) for c, route in zip(chosen[1:], routes)]
        if sweep_index == 0:
            own_hits, folds, z_folds = fold_targets(
                counts, targets, inverse_split, down, [chosen[0]]
            )
            wholes = [gathered(r, [folds]) for r in residuals]
            ready = [w[crow_size // 2] for w in wholes]
        terms = couple(info, coupling, sources, ready if sweep_index == 0 else [])
        other_terms = exchange(terms, "crow", 1)
        all_terms.append(terms)
        all_others.append(other_terms)
        if sweep_index == ITERS - 1:
            return jnp.stack(totals), add_inflow(residuals, own_hits, all_terms, all_others)
        steps, last = [], terms
        for s in range(subs):
            steps.append(
                local_solve_inflow(
                    s, inverse_split, folds, wholes[s], terms, other_terms, [last]
                )
            )
            last = steps[-1][0]
        local, residual_parts = zip(*steps)
        half = restrict(down, z_folds, residual_parts, terms, [last])
        last = half
        mine, other = spread_over_sub(half)


def solution(mesh):
    return jax.shard_map(
        per_device,
        mesh=mesh,
        in_specs=(
            P("sub", "crow", "ccol"),
            P("sub", "crow", None),
            P("sub", "crow", None),
            P("sub", None, "crow"),
            P(("sub", "crow"), None),
            P("sub", None, None, None),
            P("sub", None, None),
            P("sub", None, None),
            P("sub", None),
            P("sub"),
        ),
        out_specs=(P("sub", "crow", "ccol"), P("sub", "crow", "ccol")),
        check_vma=False,
    )
```

```python
import jax
import jax.numpy as jnp
from jax import lax
from jax.experimental import pallas as pl
from jax.experimental.pallas import tpu as pltpu
from jax.sharding import PartitionSpec as P

ITERS = 2
damping = 0.7
f32 = jnp.float32
bf16 = jnp.bfloat16
MIB = 2**20
COST = 1000.0
IN_VMEM = pl.BlockSpec(memory_space=pltpu.VMEM)
IN_SMEM = pl.BlockSpec(memory_space=pltpu.SMEM)
IN_HBM = pl.BlockSpec(memory_space=pltpu.HBM)


def call(kernel, name, operands, outputs, micros, scalars=0, scratch=(), limit=8, far=0, after=()):
    used = len(operands)

    def body(*refs):
        kernel(*refs[:used], *refs[used + len(after) :])

    operands = list(operands[: used - far]) + [
        pltpu.with_memory_space_constraint(x, pltpu.HBM) for x in operands[used - far :]
    ]
    return pl.pallas_call(
        body,
        in_specs=[IN_SMEM] * scalars
        + [IN_VMEM] * (used - scalars - far)
        + [IN_HBM] * far
        + [pl.BlockSpec(memory_space=pl.ANY)] * len(after),
        out_specs=[IN_SMEM if len(shape) == 1 else IN_VMEM for shape, _ in outputs],
        out_shape=[jax.ShapeDtypeStruct(shape, kind) for shape, kind in outputs],
        scratch_shapes=list(scratch),
        compiler_params=pltpu.CompilerParams(vmem_limit_bytes=limit * MIB),
        cost_estimate=pl.CostEstimate(flops=0, bytes_accessed=int(micros * COST), transcendentals=0),
        name=name,
    )(*operands, *after)


def position():
    crow = lax.axis_index("crow")
    return lax.axis_index("sub"), lax.rem(crow, 2), crow


def parts(x):
    hi = x.astype(bf16)
    return hi, (x - hi.astype(f32)).astype(bf16)


def beside(x):
    hi, lo = parts(x)
    return jnp.concatenate([hi, lo], axis=1)


def stacked(x):
    hi, lo = parts(x)
    return jnp.concatenate([hi, lo], axis=0)


def dot(a, b):
    return jnp.dot(a, b, preferred_element_type=f32)


def sides(product):
    columns = product.shape[1] // 2
    return product[:, :columns] + product[:, columns:]


def folded(product):
    rows = product.shape[0] // 2
    return sides(product[:rows] + product[rows:])


def exchange(x, axis, bit):
    size = lax.axis_size(axis)
    return lax.ppermute(x, axis, [(i, i ^ bit) for i in range(size) if (i ^ bit) < size])


def split_matrix(matrix, name, micros, after=()):
    subs, rows, order = matrix.shape
    tile = 96 if rows % 96 == 0 else rows
    tiles = rows // tile

    def kernel(m, o, held, sems):
        crow = lax.axis_index("crow")
        copies = [
            pltpu.make_async_copy(
                m.at[i // tiles, pl.ds((i % tiles) * tile, tile)], held.at[i], sems.at[i]
            )
            for i in range(subs * tiles)
        ]
        for copy in copies:
            copy.start()
        for i, copy in enumerate(copies):
            copy.wait()
            first = (i % tiles) * tile
            for q in range(order // rows):
                column = pl.multiple_of((crow ^ q) * rows, 128)
                hi, lo = parts(held[i, :, pl.ds(column, rows)])
                o[i // tiles, first : first + tile, q * rows : (q + 1) * rows] = hi
                o[i // tiles, rows + first : rows + first + tile, q * rows : (q + 1) * rows] = lo

    return call(
        kernel,
        name,
        [matrix],
        [((subs, 2 * rows, order), bf16)],
        micros,
        far=1,
        scratch=[
            pltpu.VMEM((subs * tiles, tile, order), f32),
            pltpu.SemaphoreType.DMA((subs * tiles,)),
        ],
        after=after,
    )[0]


def place_coarse(pieces, subs, modes, own_rows, after=()):
    height, rows = pieces[0].shape
    count = len(pieces)
    order = rows * count
    spans = (height - subs * modes) // own_rows

    def kernel(*refs):
        down, up, inverse = refs[count:]
        crow = lax.axis_index("crow")
        for q, ref in enumerate(refs[:count]):
            here = slice(q * rows, (q + 1) * rows)
            for s in range(subs):
                value = ref[s * modes : (s + 1) * modes]
                down[s, :, here] = stacked(value)
                up[s, here] = beside(value.T)
            for i in range(spans):
                first = subs * modes + i * own_rows
                inverse[crow ^ q, :, i * rows : (i + 1) * rows] = ref[first : first + own_rows]

    return call(
        kernel,
        "place_coarse",
        pieces,
        [
            ((subs, 2 * modes, order), bf16),
            ((subs, order, 2 * modes), bf16),
            ((count, own_rows, spans * rows), f32),
        ],
        1.2,
        after=after,
    )


def fold_targets(counts, targets, split, basis, after=()):
    slots, subs, width = targets.shape
    rows = split.shape[1] // 2
    order = split.shape[2]
    modes = basis.shape[1] // 2
    half = subs // 2

    def kernel(n, tg, m, z, own, folds, z_folds):
        at = position()
        line = lax.broadcasted_iota(jnp.int32, (order, width), 0)
        for s in range(subs):
            for k in range(0, slots, 2):
                pair = []
                for kk in (k, k + 1):
                    aim = in_xor_order(tg[kk, s : s + 1, :], rows, order // rows, at[2])
                    aim = jnp.where(kk < n[s], aim, -1)
                    pair.append((line == aim).astype(f32).astype(bf16))
                hit = jnp.concatenate(pair, axis=1)
                here = slice(k * width, (k + 2) * width)
                own[s, :, here] = hit[:rows]
                folds[s, :, here] = dot(m[s], hit).astype(bf16)

                @pl.when(at[1] == s // half)
                def _():
                    z_folds[s % half, :, here] = dot(z[s], hit).astype(bf16)

    return call(
        kernel,
        "fold_targets",
        [counts, targets, split, basis],
        [
            ((subs, rows, slots * width), bf16),
            ((subs, 2 * rows, slots * width), bf16),
            ((half, 2 * modes, slots * width), bf16),
        ],
        4.5,
        scalars=1,
        limit=8,
        after=after,
    )


def begin(neighbour, counts, reads, basis, residual, inverse):
    subs, modes, rows = basis.shape
    cases = residual.shape[2]
    half = subs // 2
    slots, _, width = reads.shape
    used = subs * slots
    listed = -(-(used + 2) // 8) * 8
    own_rows, columns = inverse.shape
    height = subs * modes + own_rows * (columns // rows)

    def kernel(n_far, l_far, rd_far, z_far, r_far, c_far, keep, give, r, packed, both, n, c, rd, sems):
        at = position()
        pairs = [(z_far.at[s], both.at[s * modes : (s + 1) * modes]) for s in range(subs)]
        pairs.append((r_far, r))
        for i in range(columns // rows):
            first = subs * modes + i * own_rows
            pairs.append((c_far.at[:, i * rows : (i + 1) * rows], both.at[first : first + own_rows]))
        small = [(n_far, n), (l_far, c), (rd_far, rd)]
        moves = [pltpu.make_async_copy(a, b, sems.at[i]) for i, (a, b) in enumerate(small + pairs)]
        for move in moves:
            move.start()
        for move in moves[:3]:
            move.wait()
        lane = lax.broadcasted_iota(jnp.int32, (1, width), 1)
        ids = jnp.zeros((1, width), jnp.int32)
        limits = jnp.zeros((1, width), jnp.int32)
        packed[...] = jnp.zeros((listed, width), f32)
        for s in range(subs):
            for k in range(slots):
                block = s * slots + k
                packed[block : block + 1] = rd[k, s : s + 1].astype(f32)
                ids = jnp.where(lane == block, n[s, k], ids)
                limits = jnp.where(lane == block, jnp.where(k < c[s], 1, 0), limits)
        packed[used : used + 1] = ids.astype(f32)
        packed[used + 1 : used + 2] = limits.astype(f32)
        for move in moves[3:]:
            move.wait()
        for i in range(half):
            for out, first in ((keep, at[1] * half), (give, (1 - at[1]) * half)):
                s = first + i
                z = both[pl.ds(pl.multiple_of(s * modes, modes), modes)]
                out[i * modes : (i + 1) * modes] = folded(dot(stacked(z), beside(r[s])))

    return call(
        kernel,
        "begin",
        [neighbour, counts, reads, basis, residual, inverse],
        [
            ((half * modes, cases), f32),
            ((half * modes, cases), f32),
            (residual.shape, f32),
            ((listed, width), f32),
            ((height, rows), f32),
        ],
        2.0,
        far=6,
        scratch=[
            pltpu.SMEM(neighbour.shape, jnp.int32),
            pltpu.SMEM(counts.shape, jnp.int32),
            pltpu.VMEM(reads.shape, jnp.int32),
            pltpu.SemaphoreType.DMA((subs + 4 + columns // rows,)),
        ],
    )


def relay(x, after):
    def kernel(a, b):
        b[...] = a[...]

    return call(kernel, "relay", [x], [(x.shape, x.dtype)], 0.3, after=after)[0]


def in_xor_order(rows_listed, rows, blocks, crow_index):
    block = jnp.zeros_like(rows_listed)
    for q in range(1, blocks):
        block = block + (rows_listed >= q * rows).astype(jnp.int32)
    return rows_listed + ((block ^ crow_index) - block) * rows


def prepare(held, subs, slots, rows, blocks, after=()):
    ways = len(held)
    width = held[0].shape[1]
    used = subs * slots
    half = used // 2
    listed = -(-(used + 2) // 8) * 8
    starts = [h.shape[0] - listed for h in held]

    def kernel(*refs):
        at = position()
        columns, info = refs[ways:]
        info[...] = jnp.full(info.shape, -1, jnp.int32)
        for d in range(ways):
            table = refs[d][starts[d] : starts[d] + listed].astype(jnp.int32)
            picked = jnp.where(at[1] == 0, table[:half], table[half:used])
            aims = in_xor_order(picked, rows, blocks, at[2])
            spans = lax.div(aims, width)
            within = (aims - spans * width).astype(f32)
            spans = spans.astype(f32)
            for k in range(half):
                for i, line in enumerate((within, spans)):
                    tall = jnp.broadcast_to(line[k : k + 1], (width, width)).T
                    columns[d, k, i] = tall.astype(bf16)
            ids, limits = table[used : used + 1], table[used + 1 : used + 2]
            place = ids - at[0] * subs
            use = (limits > 0) & (place >= 0) & (place < subs)
            info[d : d + 1] = jnp.where(use, place, -1)
        table = refs[0][starts[0] : starts[0] + listed].astype(jnp.int32)
        ids, limits = table[used : used + 1], table[used + 1 : used + 2]
        twin = at[0] ^ 1
        inside = (ids >= at[0] * subs) & (ids < (at[0] + 1) * subs)
        paired = (ids >= twin * subs) & (ids < (twin + 1) * subs)
        theirs = jnp.where(inside, 0, jnp.where(paired, 1, 2))
        info[ways : ways + 1] = jnp.where(limits > 0, theirs, -1)

    return call(
        kernel,
        "prepare",
        list(held),
        [((ways, half, 2, width, width), bf16), ((8, width), jnp.int32)],
        0.5,
        after=after,
    )


def add_up(a, b, below=None, after=()):
    rows = a.shape[0]
    more = 0 if below is None else below.shape[0]

    def kernel(x, y, *refs):
        o = refs[-1]
        o[:rows] = x[...] + y[...]
        if more:
            o[rows:] = refs[0][...]

    operands = [a, b] + ([] if below is None else [below])
    return call(kernel, "add_up", operands, [((rows + more, a.shape[1]), f32)], 0.2, after=after)[0]


def pile(arrays, rows, after=()):
    count = len(arrays)

    def kernel(*refs):
        for i, ref in enumerate(refs[:count]):
            refs[count][i] = ref[:rows]

    columns = arrays[0].shape[1]
    return call(kernel, "pile", arrays, [((count, rows, columns), f32)], 0.2, after=after)[0]


def load(ref, s):
    return ref[s] if len(ref.shape) == 3 else ref[...]


def local_solve(s, split, blocks, after=()):
    rows = split.shape[1] // 2
    order = split.shape[2]
    cases = blocks[0].shape[-1]

    def kernel(m, *refs):
        o, rhs = refs[-2:]
        for q, ref in enumerate(refs[:-2]):
            rhs[q * rows : (q + 1) * rows] = beside(load(ref, s))
        o[...] = folded(dot(m[s], rhs[...]))

    return call(
        kernel,
        "local_solve",
        [split, *blocks],
        [((rows, cases), f32)],
        0.8,
        scratch=[pltpu.VMEM((order, 2 * cases), bf16)],
        after=after,
    )[0]


def choose_terms(here, mine, other, terms):
    slots, width = mine.shape[:2]

    @pl.when(here)
    def _():
        for k in range(slots):
            terms[k * width : (k + 1) * width] = beside(mine[k])

    @pl.when(jnp.logical_not(here))
    def _():
        for k in range(slots):
            terms[k * width : (k + 1) * width] = beside(other[k])


def local_solve_inflow(s, split, folds, blocks, mine, other, after=()):
    rows = split.shape[1] // 2
    order = split.shape[2]
    subs = split.shape[0]
    cases = blocks[0].shape[-1]
    slots, width = mine.shape[:2]
    count = len(blocks)

    def kernel(m, f, g_mine, g_other, *refs):
        at = position()
        o, rhs, terms = refs[count:]
        for q, ref in enumerate(refs[:count]):
            rhs[q * rows : (q + 1) * rows] = beside(load(ref, s))
        choose_terms(at[1] == s // (subs // 2), g_mine, g_other, terms)
        o[...] = folded(dot(m[s], rhs[...])) + damping * folded(dot(f[s], terms[...]))

    return call(
        kernel,
        "local_solve_inflow",
        [split, folds, mine, other, *blocks],
        [((rows, cases), f32), ((order, 2 * cases), bf16)],
        1.2,
        scratch=[pltpu.VMEM((slots * width, 2 * cases), bf16)],
        after=after,
    )


def restrict(basis, z_folds, residual_parts, terms, after=()):
    subs = basis.shape[0]
    modes = basis.shape[1] // 2
    cases = residual_parts[0].shape[1] // 2
    half = subs // 2
    slots, width = terms.shape[0] // half, terms.shape[1]

    def kernel(z, zf, g, *refs):
        at = position()
        out, rhs = refs[subs:]
        for i in range(half):
            for k in range(slots):
                rhs[k * width : (k + 1) * width] = beside(g[i * slots + k])
            inflow = damping * folded(dot(zf[i], rhs[...]))
            for s in range(i, subs, half):

                @pl.when(at[1] == s // half)
                def _():
                    out[i * modes : (i + 1) * modes] = folded(dot(z[s], refs[s][...])) + inflow

    return call(
        kernel,
        "restrict",
        [basis, z_folds, terms, *residual_parts],
        [((half * modes, cases), f32)],
        0.4,
        scratch=[pltpu.VMEM((slots * width, 2 * cases), bf16)],
        after=after,
    )[0]


def lift_coarse(inverse, lift, mine, other, after=()):
    subs, order, twice = lift.shape
    modes = twice // 2
    groups, _, cases = mine.shape
    half = subs // 2
    per_sub = inverse.shape[0] // subs
    columns = inverse.shape[2]

    def kernel(c, z, g_mine, g_other, o, right):
        at = position()
        for b in range(groups):
            base = (at[0] ^ b) * (2 * half * modes)
            for h, ref in ((at[1], g_mine), (1 - at[1], g_other)):
                row = pl.multiple_of(base + h * (half * modes), 16)
                right[pl.ds(row, half * modes)] = beside(ref[b])
        for s in range(subs):
            c_rows = c[s * per_sub : (s + 1) * per_sub].reshape(modes, columns)
            coarse = beside(folded(dot(stacked(c_rows), right[...])))
            o[s] = sides(dot(z[s], jnp.concatenate([coarse, coarse], axis=0)))

    return call(
        kernel,
        "lift_coarse",
        [inverse, lift, mine, other],
        [((subs, order, cases), f32)],
        1.2,
        scratch=[pltpu.VMEM((columns, 2 * cases), bf16)],
        limit=16,
        after=after,
    )[0]


def correct(lifted, blocks, old, info, lists, after=()):
    subs = len(blocks)
    count = len(blocks[0])
    rows, cases = blocks[0][0].shape
    order = rows * count
    ways, slots, _, width, _ = lists.shape
    has_old = old is not None

    def kernel(up, facts, l, *refs):
        block_refs = refs[: subs * count]
        refs = refs[subs * count :]
        old_ref, refs = (refs[0], refs[1:]) if has_old else (None, refs)
        total, corrs, outs = refs[0], refs[1 : 1 + subs], refs[1 + subs : 1 + subs + ways]
        where, sem = refs[1 + subs + ways :]
        move = pltpu.make_async_copy(facts, where, sem)
        move.start()
        core = position()[1]
        for s in range(subs):
            for q in range(count):
                here = slice(q * rows, (q + 1) * rows)
                value = block_refs[s * count + q][...] + up[s, here]
                corrs[s][here] = beside(value)
                if q == 0:
                    total[s] = damping * value + old_ref[s] if has_old else damping * value
        move.wait()
        lane = lax.broadcasted_iota(jnp.int32, (width, width), 1).astype(f32).astype(bf16)
        none = jnp.zeros((width, width), bf16)
        for d in range(ways):

            @pl.loop(0, slots)
            def _(k):
                place = where[d, core * slots + k]

                @pl.when(place < 0)
                def _():
                    outs[d][k] = jnp.zeros((width, cases), f32)

                for s in range(subs):

                    @pl.when(place == s)
                    def _():
                        one = jnp.where(l[d, k, 0] == lane, jnp.ones_like(none), none)
                        span = l[d, k, 1]
                        ones = [jnp.where(span == t, one, none) for t in range(order // width)]
                        outs[d][k] = sides(dot(jnp.concatenate(ones, axis=1), corrs[s][...]))

    flat = [b for of_sub in blocks for b in of_sub]
    return call(
        kernel,
        "correct",
        [lifted, info, lists, *flat] + ([old] if has_old else []),
        [((subs, rows, cases), f32)]
        + [((order, 2 * cases), bf16)] * subs
        + [((slots, width, cases), f32)] * ways,
        3.0,
        scratch=[pltpu.SMEM(info.shape, jnp.int32), pltpu.SemaphoreType.DMA(())],
        after=after,
    )


def reduce_residual(split, corrs, residual, after=()):
    subs, rows, cases = residual.shape

    def kernel(m, res, *refs):
        for s in range(subs):
            refs[subs][s] = res[s] - damping * folded(dot(m[s], refs[s][...]))

    return call(
        kernel,
        "reduce_residual",
        [split, residual, *corrs],
        [(residual.shape, f32)],
        1.2,
        after=after,
    )[0]


def couple(info, coupling, sources, after=()):
    subs, per_sub, width, _ = coupling.shape
    slots, _, cases = sources[0].shape
    ways = len(sources)

    def kernel(facts, c, *refs):
        out, left, right, where, sem = refs[ways:]
        move = pltpu.make_async_copy(facts, where, sem)
        move.start()
        first = position()[1] * slots
        for k in range(slots):
            block = first + k
            left[k] = stacked(c[block // per_sub, lax.rem(block, per_sub)])
        move.wait()
        for k in range(slots):
            code = where[ways, first + k]

            @pl.when(code < 0)
            def _():
                right[k] = jnp.zeros((width, 2 * cases), bf16)

            for d, ref in enumerate(refs[:ways]):

                @pl.when(code == d)
                def _():
                    right[k] = beside(ref[k])

        for k in range(slots):
            out[k] = folded(dot(left[k], right[k]))

    return call(
        kernel,
        "couple",
        [info, coupling, *sources],
        [((slots, width, cases), f32)],
        0.8,
        scratch=[
            pltpu.VMEM((slots, 2 * width, width), bf16),
            pltpu.VMEM((slots, width, 2 * cases), bf16),
            pltpu.SMEM(info.shape, jnp.int32),
            pltpu.SemaphoreType.DMA(()),
        ],
        after=after,
    )[0]


def add_own_half(residual, hits, terms, old=None, after=()):
    subs, rows, cases = residual.shape
    slots, width, _ = terms.shape
    half = subs // 2
    per_sub = slots // half

    def kernel(res, tg, g, *refs):
        out, rhs = refs[-2:]
        core = position()[1]
        side = core if old is None else 1 - core
        for i in range(half):
            for k in range(per_sub):
                rhs[k * width : (k + 1) * width] = beside(g[i * per_sub + k])
            s = side * half + i
            value = res[s] + damping * sides(dot(tg[s], rhs[...]))
            if old is None:
                out[i] = value
            else:
                out[s] = value
                out[core * half + i] = refs[0][i]

    return call(
        kernel,
        "add_own_half",
        [residual, hits, terms] + ([] if old is None else [old]),
        [((half if old is None else subs, rows, cases), f32)],
        0.8,
        scratch=[pltpu.VMEM((per_sub * width, 2 * cases), bf16)],
        after=after,
    )[0]


def add_inflow(residual, hits, terms, others, after=()):
    own = add_own_half(residual, hits, terms, None, after)
    return add_own_half(residual, hits, others, own)


def gathered(x, hold=()):
    bit = lax.axis_size("crow") // 2
    blocks = {0: x}
    while bit >= 1:
        news = {q | bit: exchange(b, "crow", bit) for q, b in blocks.items()}
        if bit > 1 and hold:
            news = {q: relay(b, hold) for q, b in news.items()}
        blocks.update(news)
        bit //= 2
    return [blocks[q] for q in sorted(blocks)]


def spread_over_sub(half):
    return [half] + [exchange(half, "sub", b) for b in range(1, lax.axis_size("sub"))]


def pair_routes(size):
    low = [(i, i + 1) for i in range(0, size - 1, 2)]
    high = [(i, i + 1) for i in range(1, size - 1, 2)]
    return [[p for a, b in pairs for p in ((a, b), (b, a))] for pairs in (low, high)]


def per_device(
    load_cases,
    stiffness,
    local_inverse,
    coarse_basis,
    coarse_inverse,
    coupling,
    target_local_rows,
    neighbour_read_rows,
    neighbour,
    counts,
):
    subs, rows, cases = load_cases.shape
    slots = neighbour.shape[1]
    groups = lax.axis_size("sub")
    crow_size = lax.axis_size("crow")
    targets = target_local_rows.transpose(1, 0, 2)
    routes = pair_routes(groups)

    keep, give, residual, packed, both = begin(
        neighbour, counts, neighbour_read_rows.transpose(1, 0, 2), coarse_basis, load_cases,
        coarse_inverse,
    )
    keep = add_up(keep, exchange(give, "crow", 1))
    inverse_split = split_matrix(local_inverse, "split_inverse", 2.0, [keep])
    bits = [bit for bit in (2, 4, 8) if bit < crow_size]
    for bit in bits[:-1]:
        keep = add_up(keep, exchange(keep, "crow", bit), None, [inverse_split])
    more = relay(exchange(keep, "crow", bits[-1]), [inverse_split])
    first_blocks = gathered(load_cases, [more])
    both = relay(both, [more])
    local = []
    for s in range(subs):
        local.append(local_solve(s, inverse_split, first_blocks, local[-1:]))
    stiffness_split = split_matrix(stiffness, "split_stiffness", 9000.0, [local[-1]])
    local_blocks = [gathered(v, [stiffness_split]) for v in local]
    arrived = [b[crow_size // 2] for b in local_blocks]

    halves = spread_over_sub(add_up(keep, more, packed, [stiffness_split]))
    height = give.shape[0]
    mine = pile(halves, height, arrived)
    other = exchange(mine, "crow", 1)
    pieces = gathered(both, [mine])
    down, lift, inverse = place_coarse(
        pieces, subs, coarse_basis.shape[1], coarse_inverse.shape[0], [mine]
    )

    if groups == 4:
        held = [packed, halves[1], halves[3]]
    else:
        held = [packed] + [lax.ppermute(packed, "sub", route) for route in routes]
    lists, info = prepare(held, subs, slots, rows, crow_size, [down])

    total, last = None, info
    for sweep_index in range(ITERS):
        if sweep_index:
            local_blocks = [gathered(v) for v in local]
        lifted = lift_coarse(inverse, lift, mine, other, [last])
        total, *rest = correct(lifted, local_blocks, total, info, lists)
        corrs, chosen = rest[:subs], rest[subs:]
        sources = [chosen[0]] + [lax.ppermute(c, "sub", route) for c, route in zip(chosen[1:], routes)]
        residual = reduce_residual(stiffness_split, corrs, residual)
        if sweep_index == 0:
            own_hits, folds, z_folds = fold_targets(
                counts, targets, inverse_split, down, [residual]
            )
            whole = gathered(residual, [folds])
            ready = [folds]
        else:
            residual = add_inflow(residual, own_hits, *held_terms, [residual])
            ready = [residual]
        terms = couple(info, coupling, sources, ready)
        other_terms = exchange(terms, "crow", 1)
        held_terms = (terms, other_terms)
        if sweep_index == ITERS - 1:
            return total, add_inflow(residual, own_hits, terms, other_terms)
        steps, last = [], terms
        for s in range(subs):
            steps.append(local_solve_inflow(s, inverse_split, folds, whole, terms, other_terms, [last]))
            last = steps[-1][0]
        local, residual_parts = zip(*steps)
        half = restrict(down, z_folds, residual_parts, terms, [last])
        mine = pile(spread_over_sub(half), height)
        other = exchange(mine, "crow", 1)
        last = mine


def solution(mesh):
    return jax.shard_map(
        per_device,
        mesh=mesh,
        in_specs=(
            P("sub", "crow", "ccol"),
            P("sub", "crow", None),
            P("sub", "crow", None),
            P("sub", None, "crow"),
            P(("sub", "crow"), None),
            P("sub", None, None, None),
            P("sub", None, None),
            P("sub", None, None),
            P("sub", None),
            P("sub"),
        ),
        out_specs=(P("sub", "crow", "ccol"), P("sub", "crow", "ccol")),
        check_vma=False,
    )
```

```python
import jax
import jax.numpy as jnp
from jax import lax
from jax.experimental import pallas as pl
from jax.experimental.pallas import tpu as pltpu
from jax.sharding import PartitionSpec as P

ITERS = 2
damping = 0.7
f32 = jnp.float32
bf16 = jnp.bfloat16
MIB = 2**20
COST = 1000.0
IN_VMEM = pl.BlockSpec(memory_space=pltpu.VMEM)
IN_SMEM = pl.BlockSpec(memory_space=pltpu.SMEM)
IN_HBM = pl.BlockSpec(memory_space=pltpu.HBM)


def call(kernel, name, operands, outputs, micros, scalars=0, scratch=(), limit=8, far=0, after=()):
    used = len(operands)

    def body(*refs):
        kernel(*refs[:used], *refs[used + len(after) :])

    operands = list(operands[: used - far]) + [
        pltpu.with_memory_space_constraint(x, pltpu.HBM) for x in operands[used - far :]
    ]
    return pl.pallas_call(
        body,
        in_specs=[IN_SMEM] * scalars
        + [IN_VMEM] * (used - scalars - far)
        + [IN_HBM] * far
        + [pl.BlockSpec(memory_space=pl.ANY)] * len(after),
        out_specs=[IN_SMEM if len(shape) == 1 else IN_VMEM for shape, _ in outputs],
        out_shape=[jax.ShapeDtypeStruct(shape, kind) for shape, kind in outputs],
        scratch_shapes=list(scratch),
        compiler_params=pltpu.CompilerParams(vmem_limit_bytes=limit * MIB),
        cost_estimate=pl.CostEstimate(flops=0, bytes_accessed=int(micros * COST), transcendentals=0),
        name=name,
    )(*operands, *after)


def position():
    crow = lax.axis_index("crow")
    return lax.axis_index("sub"), lax.rem(crow, 2), crow


def parts(x):
    hi = x.astype(bf16)
    return hi, (x - hi.astype(f32)).astype(bf16)


def beside(x):
    hi, lo = parts(x)
    return jnp.concatenate([hi, lo], axis=1)


def stacked(x):
    hi, lo = parts(x)
    return jnp.concatenate([hi, lo], axis=0)


def dot(a, b):
    return jnp.dot(a, b, preferred_element_type=f32)


def sides(product):
    columns = product.shape[1] // 2
    return product[:, :columns] + product[:, columns:]


def folded(product):
    rows = product.shape[0] // 2
    return sides(product[:rows] + product[rows:])


def exchange(x, axis, bit):
    size = lax.axis_size(axis)
    return lax.ppermute(x, axis, [(i, i ^ bit) for i in range(size) if (i ^ bit) < size])


def split_matrix(matrix, name, micros, after=()):
    subs, rows, order = matrix.shape
    tile = 96 if rows % 96 == 0 else rows
    tiles = rows // tile

    def kernel(m, o, held, sems):
        crow = lax.axis_index("crow")
        copies = [
            pltpu.make_async_copy(
                m.at[i // tiles, pl.ds((i % tiles) * tile, tile)], held.at[i], sems.at[i]
            )
            for i in range(subs * tiles)
        ]
        for copy in copies:
            copy.start()
        for i, copy in enumerate(copies):
            copy.wait()
            first = (i % tiles) * tile
            for q in range(order // rows):
                column = pl.multiple_of((crow ^ q) * rows, 128)
                hi, lo = parts(held[i, :, pl.ds(column, rows)])
                o[i // tiles, first : first + tile, q * rows : (q + 1) * rows] = hi
                o[i // tiles, rows + first : rows + first + tile, q * rows : (q + 1) * rows] = lo

    return call(
        kernel,
        name,
        [matrix],
        [((subs, 2 * rows, order), bf16)],
        micros,
        far=1,
        scratch=[
            pltpu.VMEM((subs * tiles, tile, order), f32),
            pltpu.SemaphoreType.DMA((subs * tiles,)),
        ],
        after=after,
    )[0]


def place_coarse(pieces, subs, modes, own_rows, after=()):
    height, rows = pieces[0].shape
    count = len(pieces)
    order = rows * count
    spans = (height - subs * modes) // own_rows

    def kernel(*refs):
        down, up, inverse = refs[count:]
        crow = lax.axis_index("crow")
        for q, ref in enumerate(refs[:count]):
            here = slice(q * rows, (q + 1) * rows)
            for s in range(subs):
                value = ref[s * modes : (s + 1) * modes]
                down[s, :, here] = stacked(value)
                up[s, here] = beside(value.T)
            for i in range(spans):
                first = subs * modes + i * own_rows
                inverse[crow ^ q, :, i * rows : (i + 1) * rows] = ref[first : first + own_rows]

    return call(
        kernel,
        "place_coarse",
        pieces,
        [
            ((subs, 2 * modes, order), bf16),
            ((subs, order, 2 * modes), bf16),
            ((count, own_rows, spans * rows), f32),
        ],
        1.2,
        after=after,
    )


def fold_targets(counts, targets, split, basis, after=()):
    slots, subs, width = targets.shape
    rows = split.shape[1] // 2
    order = split.shape[2]
    modes = basis.shape[1] // 2
    half = subs // 2

    def kernel(n, tg, m, z, own, folds, z_folds):
        at = position()
        line = lax.broadcasted_iota(jnp.int32, (order, width), 0)
        for s in range(subs):
            for k in range(0, slots, 2):
                pair = []
                for kk in (k, k + 1):
                    aim = in_xor_order(tg[kk, s : s + 1, :], rows, order // rows, at[2])
                    aim = jnp.where(kk < n[s], aim, -1)
                    pair.append((line == aim).astype(f32).astype(bf16))
                hit = jnp.concatenate(pair, axis=1)
                here = slice(k * width, (k + 2) * width)
                own[s, :, here] = hit[:rows]
                folds[s, :, here] = dot(m[s], hit).astype(bf16)

                @pl.when(at[1] == s // half)
                def _():
                    z_folds[s % half, :, here] = dot(z[s], hit).astype(bf16)

    return call(
        kernel,
        "fold_targets",
        [counts, targets, split, basis],
        [
            ((subs, rows, slots * width), bf16),
            ((subs, 2 * rows, slots * width), bf16),
            ((half, 2 * modes, slots * width), bf16),
        ],
        4.5,
        scalars=1,
        limit=8,
        after=after,
    )


def begin(neighbour, counts, reads, basis, residual, inverse):
    subs, modes, rows = basis.shape
    cases = residual.shape[2]
    half = subs // 2
    slots, _, width = reads.shape
    used = subs * slots
    listed = -(-(used + 2) // 8) * 8
    own_rows, columns = inverse.shape
    height = subs * modes + own_rows * (columns // rows)

    def kernel(n_far, l_far, rd_far, z_far, r_far, c_far, keep, give, r, packed, both, n, c, rd, sems):
        at = position()
        pairs = [(z_far.at[s], both.at[s * modes : (s + 1) * modes]) for s in range(subs)]
        pairs.append((r_far, r))
        for i in range(columns // rows):
            first = subs * modes + i * own_rows
            pairs.append((c_far.at[:, i * rows : (i + 1) * rows], both.at[first : first + own_rows]))
        small = [(n_far, n), (l_far, c), (rd_far, rd)]
        moves = [pltpu.make_async_copy(a, b, sems.at[i]) for i, (a, b) in enumerate(small + pairs)]
        for move in moves:
            move.start()
        for move in moves[:3]:
            move.wait()
        lane = lax.broadcasted_iota(jnp.int32, (1, width), 1)
        ids = jnp.zeros((1, width), jnp.int32)
        limits = jnp.zeros((1, width), jnp.int32)
        packed[...] = jnp.zeros((listed, width), f32)
        for s in range(subs):
            for k in range(slots):
                block = s * slots + k
                packed[block : block + 1] = rd[k, s : s + 1].astype(f32)
                ids = jnp.where(lane == block, n[s, k], ids)
                limits = jnp.where(lane == block, jnp.where(k < c[s], 1, 0), limits)
        packed[used : used + 1] = ids.astype(f32)
        packed[used + 1 : used + 2] = limits.astype(f32)
        for move in moves[3:]:
            move.wait()
        for i in range(half):
            for out, first in ((keep, at[1] * half), (give, (1 - at[1]) * half)):
                s = first + i
                z = both[pl.ds(pl.multiple_of(s * modes, modes), modes)]
                out[i * modes : (i + 1) * modes] = folded(dot(stacked(z), beside(r[s])))

    return call(
        kernel,
        "begin",
        [neighbour, counts, reads, basis, residual, inverse],
        [
            ((half * modes, cases), f32),
            ((half * modes, cases), f32),
            (residual.shape, f32),
            ((listed, width), f32),
            ((height, rows), f32),
        ],
        2.0,
        far=6,
        scratch=[
            pltpu.SMEM(neighbour.shape, jnp.int32),
            pltpu.SMEM(counts.shape, jnp.int32),
            pltpu.VMEM(reads.shape, jnp.int32),
            pltpu.SemaphoreType.DMA((subs + 4 + columns // rows,)),
        ],
    )


def relay(x, after):
    def kernel(a, b):
        b[...] = a[...]

    return call(kernel, "relay", [x], [(x.shape, x.dtype)], 0.3, after=after)[0]


def in_xor_order(rows_listed, rows, blocks, crow_index):
    block = jnp.zeros_like(rows_listed)
    for q in range(1, blocks):
        block = block + (rows_listed >= q * rows).astype(jnp.int32)
    return rows_listed + ((block ^ crow_index) - block) * rows


def prepare(held, subs, slots, rows, blocks, after=()):
    ways = len(held)
    width = held[0].shape[1]
    used = subs * slots
    half = used // 2
    listed = -(-(used + 2) // 8) * 8
    starts = [h.shape[0] - listed for h in held]

    def kernel(*refs):
        at = position()
        columns, info = refs[ways:]
        info[...] = jnp.full(info.shape, -1, jnp.int32)
        for d in range(ways):
            table = refs[d][starts[d] : starts[d] + listed].astype(jnp.int32)
            picked = jnp.where(at[1] == 0, table[:half], table[half:used])
            aims = in_xor_order(picked, rows, blocks, at[2])
            spans = lax.div(aims, width)
            within = (aims - spans * width).astype(f32)
            spans = spans.astype(f32)
            for k in range(half):
                for i, line in enumerate((within, spans)):
                    tall = jnp.broadcast_to(line[k : k + 1], (width, width)).T
                    columns[d, k, i] = tall.astype(bf16)
            ids, limits = table[used : used + 1], table[used + 1 : used + 2]
            place = ids - at[0] * subs
            use = (limits > 0) & (place >= 0) & (place < subs)
            info[d : d + 1] = jnp.where(use, place, -1)
        table = refs[0][starts[0] : starts[0] + listed].astype(jnp.int32)
        ids, limits = table[used : used + 1], table[used + 1 : used + 2]
        twin = at[0] ^ 1
        inside = (ids >= at[0] * subs) & (ids < (at[0] + 1) * subs)
        paired = (ids >= twin * subs) & (ids < (twin + 1) * subs)
        theirs = jnp.where(inside, 0, jnp.where(paired, 1, 2))
        info[ways : ways + 1] = jnp.where(limits > 0, theirs, -1)

    return call(
        kernel,
        "prepare",
        list(held),
        [((ways, half, 2, width, width), bf16), ((8, width), jnp.int32)],
        0.5,
        after=after,
    )


def add_up(a, b, below=None, after=()):
    rows = a.shape[0]
    more = 0 if below is None else below.shape[0]

    def kernel(x, y, *refs):
        o = refs[-1]
        o[:rows] = x[...] + y[...]
        if more:
            o[rows:] = refs[0][...]

    operands = [a, b] + ([] if below is None else [below])
    return call(kernel, "add_up", operands, [((rows + more, a.shape[1]), f32)], 0.2, after=after)[0]


def pile(arrays, rows, after=()):
    count = len(arrays)

    def kernel(*refs):
        for i, ref in enumerate(refs[:count]):
            refs[count][i] = ref[:rows]

    columns = arrays[0].shape[1]
    return call(kernel, "pile", arrays, [((count, rows, columns), f32)], 0.2, after=after)[0]


def load(ref, s):
    return ref[s] if len(ref.shape) == 3 else ref[...]


def local_solve(s, split, blocks, after=()):
    rows = split.shape[1] // 2
    order = split.shape[2]
    cases = blocks[0].shape[-1]

    def kernel(m, *refs):
        o, rhs = refs[-2:]
        for q, ref in enumerate(refs[:-2]):
            rhs[q * rows : (q + 1) * rows] = beside(load(ref, s))
        o[...] = folded(dot(m[s], rhs[...]))

    return call(
        kernel,
        "local_solve",
        [split, *blocks],
        [((rows, cases), f32)],
        0.8,
        scratch=[pltpu.VMEM((order, 2 * cases), bf16)],
        after=after,
    )[0]


def choose_terms(here, mine, other, terms):
    slots, width = mine.shape[:2]

    @pl.when(here)
    def _():
        for k in range(slots):
            terms[k * width : (k + 1) * width] = beside(mine[k])

    @pl.when(jnp.logical_not(here))
    def _():
        for k in range(slots):
            terms[k * width : (k + 1) * width] = beside(other[k])


def local_solve_inflow(s, split, folds, blocks, mine, other, after=()):
    rows = split.shape[1] // 2
    order = split.shape[2]
    subs = split.shape[0]
    cases = blocks[0].shape[-1]
    slots, width = mine.shape[:2]
    count = len(blocks)

    def kernel(m, f, g_mine, g_other, *refs):
        at = position()
        o, rhs, terms = refs[count:]
        for q, ref in enumerate(refs[:count]):
            rhs[q * rows : (q + 1) * rows] = beside(load(ref, s))
        choose_terms(at[1] == s // (subs // 2), g_mine, g_other, terms)
        o[...] = folded(dot(m[s], rhs[...])) + damping * folded(dot(f[s], terms[...]))

    return call(
        kernel,
        "local_solve_inflow",
        [split, folds, mine, other, *blocks],
        [((rows, cases), f32), ((order, 2 * cases), bf16)],
        1.2,
        scratch=[pltpu.VMEM((slots * width, 2 * cases), bf16)],
        after=after,
    )


def restrict(basis, z_folds, residual_parts, terms, after=()):
    subs = basis.shape[0]
    modes = basis.shape[1] // 2
    cases = residual_parts[0].shape[1] // 2
    half = subs // 2
    slots, width = terms.shape[0] // half, terms.shape[1]

    def kernel(z, zf, g, *refs):
        at = position()
        out, rhs = refs[subs:]
        for i in range(half):
            for k in range(slots):
                rhs[k * width : (k + 1) * width] = beside(g[i * slots + k])
            inflow = damping * folded(dot(zf[i], rhs[...]))
            for s in range(i, subs, half):

                @pl.when(at[1] == s // half)
                def _():
                    out[i * modes : (i + 1) * modes] = folded(dot(z[s], refs[s][...])) + inflow

    return call(
        kernel,
        "restrict",
        [basis, z_folds, terms, *residual_parts],
        [((half * modes, cases), f32)],
        0.4,
        scratch=[pltpu.VMEM((slots * width, 2 * cases), bf16)],
        after=after,
    )[0]


def lift_coarse(inverse, lift, mine, other, after=()):
    subs, order, twice = lift.shape
    modes = twice // 2
    groups, _, cases = mine.shape
    half = subs // 2
    per_sub = inverse.shape[0] // subs
    columns = inverse.shape[2]

    def kernel(c, z, g_mine, g_other, o, right):
        at = position()
        for b in range(groups):
            base = (at[0] ^ b) * (2 * half * modes)
            for h, ref in ((at[1], g_mine), (1 - at[1], g_other)):
                row = pl.multiple_of(base + h * (half * modes), 16)
                right[pl.ds(row, half * modes)] = beside(ref[b])
        for s in range(subs):
            c_rows = c[s * per_sub : (s + 1) * per_sub].reshape(modes, columns)
            coarse = beside(folded(dot(stacked(c_rows), right[...])))
            o[s] = sides(dot(z[s], jnp.concatenate([coarse, coarse], axis=0)))

    return call(
        kernel,
        "lift_coarse",
        [inverse, lift, mine, other],
        [((subs, order, cases), f32)],
        1.2,
        scratch=[pltpu.VMEM((columns, 2 * cases), bf16)],
        limit=16,
        after=after,
    )[0]


def correct(lifted, blocks, info, lists, after=()):
    subs = len(blocks)
    count = len(blocks[0])
    rows, cases = blocks[0][0].shape
    order = rows * count
    ways, slots, _, width, _ = lists.shape

    def kernel(up, facts, l, *refs):
        block_refs = refs[: subs * count]
        refs = refs[subs * count :]
        corrs, outs = refs[:subs], refs[subs : subs + ways]
        where, sem = refs[subs + ways :]
        move = pltpu.make_async_copy(facts, where, sem)
        move.start()
        core = position()[1]
        for s in range(subs):
            for q in range(count):
                here = slice(q * rows, (q + 1) * rows)
                value = block_refs[s * count + q][...] + up[s, here]
                corrs[s][here] = beside(value)
        move.wait()
        lane = lax.broadcasted_iota(jnp.int32, (width, width), 1).astype(f32).astype(bf16)
        none = jnp.zeros((width, width), bf16)
        for d in range(ways):

            @pl.loop(0, slots)
            def _(k):
                place = where[d, core * slots + k]

                @pl.when(place < 0)
                def _():
                    outs[d][k] = jnp.zeros((width, cases), f32)

                for s in range(subs):

                    @pl.when(place == s)
                    def _():
                        one = jnp.where(l[d, k, 0] == lane, jnp.ones_like(none), none)
                        span = l[d, k, 1]
                        ones = [jnp.where(span == t, one, none) for t in range(order // width)]
                        outs[d][k] = sides(dot(jnp.concatenate(ones, axis=1), corrs[s][...]))

    flat = [b for of_sub in blocks for b in of_sub]
    return call(
        kernel,
        "correct",
        [lifted, info, lists, *flat],
        [((order, 2 * cases), bf16)] * subs
        + [((slots, width, cases), f32)] * ways,
        3.0,
        scratch=[pltpu.SMEM(info.shape, jnp.int32), pltpu.SemaphoreType.DMA(())],
        after=after,
    )


def reduce_residual(split, corrs, residual, lifted, own, old=None, after=()):
    subs, rows, cases = residual.shape

    def kernel(m, res, up, *refs):
        o, total = refs[-2:]
        for s in range(subs):
            o[s] = res[s] - damping * folded(dot(m[s], refs[s][...]))
            value = damping * (refs[subs + s][...] + up[s, :rows])
            total[s] = value if old is None else refs[2 * subs][s] + value

    return call(
        kernel,
        "reduce_residual",
        [split, residual, lifted, *corrs, *own] + ([] if old is None else [old]),
        [(residual.shape, f32), (residual.shape, f32)],
        1.2,
        after=after,
    )


def couple(info, coupling, sources, after=()):
    subs, per_sub, width, _ = coupling.shape
    slots, _, cases = sources[0].shape
    ways = len(sources)

    def kernel(facts, c, *refs):
        out, left, right, where, sem = refs[ways:]
        move = pltpu.make_async_copy(facts, where, sem)
        move.start()
        first = position()[1] * slots
        for k in range(slots):
            block = first + k
            left[k] = stacked(c[block // per_sub, lax.rem(block, per_sub)])
        move.wait()
        for k in range(slots):
            code = where[ways, first + k]

            @pl.when(code < 0)
            def _():
                right[k] = jnp.zeros((width, 2 * cases), bf16)

            for d, ref in enumerate(refs[:ways]):

                @pl.when(code == d)
                def _():
                    right[k] = beside(ref[k])

        for k in range(slots):
            out[k] = folded(dot(left[k], right[k]))

    return call(
        kernel,
        "couple",
        [info, coupling, *sources],
        [((slots, width, cases), f32)],
        0.8,
        scratch=[
            pltpu.VMEM((slots, 2 * width, width), bf16),
            pltpu.VMEM((slots, width, 2 * cases), bf16),
            pltpu.SMEM(info.shape, jnp.int32),
            pltpu.SemaphoreType.DMA(()),
        ],
        after=after,
    )[0]


def add_own_half(residual, hits, terms, old=None, after=()):
    subs, rows, cases = residual.shape
    slots, width, _ = terms.shape
    half = subs // 2
    per_sub = slots // half

    def kernel(res, tg, g, *refs):
        out, rhs = refs[-2:]
        core = position()[1]
        side = core if old is None else 1 - core
        for i in range(half):
            for k in range(per_sub):
                rhs[k * width : (k + 1) * width] = beside(g[i * per_sub + k])
            s = side * half + i
            value = res[s] + damping * sides(dot(tg[s], rhs[...]))
            if old is None:
                out[i] = value
            else:
                out[s] = value
                out[core * half + i] = refs[0][i]

    return call(
        kernel,
        "add_own_half",
        [residual, hits, terms] + ([] if old is None else [old]),
        [((half if old is None else subs, rows, cases), f32)],
        0.8,
        scratch=[pltpu.VMEM((per_sub * width, 2 * cases), bf16)],
        after=after,
    )[0]


def add_inflow(residual, hits, terms, others, after=()):
    own = add_own_half(residual, hits, terms, None, after)
    return add_own_half(residual, hits, others, own)


def gathered(x, hold=()):
    bit = lax.axis_size("crow") // 2
    blocks = {0: x}
    while bit >= 1:
        news = {q | bit: exchange(b, "crow", bit) for q, b in blocks.items()}
        if bit > 1 and hold:
            news = {q: relay(b, hold) for q, b in news.items()}
        blocks.update(news)
        bit //= 2
    return [blocks[q] for q in sorted(blocks)]


def spread_over_sub(half):
    return [half] + [exchange(half, "sub", b) for b in range(1, lax.axis_size("sub"))]


def pair_routes(size):
    low = [(i, i + 1) for i in range(0, size - 1, 2)]
    high = [(i, i + 1) for i in range(1, size - 1, 2)]
    return [[p for a, b in pairs for p in ((a, b), (b, a))] for pairs in (low, high)]


def per_device(
    load_cases,
    stiffness,
    local_inverse,
    coarse_basis,
    coarse_inverse,
    coupling,
    target_local_rows,
    neighbour_read_rows,
    neighbour,
    counts,
):
    subs, rows, cases = load_cases.shape
    slots = neighbour.shape[1]
    groups = lax.axis_size("sub")
    crow_size = lax.axis_size("crow")
    targets = target_local_rows.transpose(1, 0, 2)
    routes = pair_routes(groups)

    keep, give, residual, packed, both = begin(
        neighbour, counts, neighbour_read_rows.transpose(1, 0, 2), coarse_basis, load_cases,
        coarse_inverse,
    )
    keep = add_up(keep, exchange(give, "crow", 1))
    inverse_split = split_matrix(local_inverse, "split_inverse", 2.0, [keep])
    bits = [bit for bit in (2, 4, 8) if bit < crow_size]
    for bit in bits[:-1]:
        keep = add_up(keep, exchange(keep, "crow", bit), None, [inverse_split])
    more = relay(exchange(keep, "crow", bits[-1]), [inverse_split])
    first_blocks = gathered(load_cases, [more])
    both = relay(both, [more])
    local = []
    for s in range(subs):
        local.append(local_solve(s, inverse_split, first_blocks, local[-1:]))
    stiffness_split = split_matrix(stiffness, "split_stiffness", 9000.0, [local[-1]])
    local_blocks = [gathered(v, [stiffness_split]) for v in local]
    arrived = [b[crow_size // 2] for b in local_blocks]

    halves = spread_over_sub(add_up(keep, more, packed, [stiffness_split]))
    height = give.shape[0]
    mine = pile(halves, height, arrived)
    other = exchange(mine, "crow", 1)
    pieces = gathered(both, [mine])
    if groups == 4:
        held = [packed, halves[1], halves[3]]
    else:
        held = [packed] + [lax.ppermute(packed, "sub", route) for route in routes]
    lists, info = prepare(held, subs, slots, rows, crow_size, [mine])
    down, lift, inverse = place_coarse(
        pieces, subs, coarse_basis.shape[1], coarse_inverse.shape[0], [info]
    )

    total, last = None, down
    for sweep_index in range(ITERS):
        if sweep_index:
            local_blocks = [gathered(v) for v in local]
        lifted = lift_coarse(inverse, lift, mine, other, [last])
        rest = correct(lifted, local_blocks, info, lists)
        corrs, chosen = rest[:subs], rest[subs:]
        sources = [chosen[0]] + [lax.ppermute(c, "sub", route) for c, route in zip(chosen[1:], routes)]
        own = [blocks[0] for blocks in local_blocks]
        residual, total = reduce_residual(stiffness_split, corrs, residual, lifted, own, total)
        if sweep_index == 0:
            own_hits, folds, z_folds = fold_targets(
                counts, targets, inverse_split, down, [residual]
            )
            whole = gathered(residual, [folds])
            ready = [folds]
        else:
            residual = add_inflow(residual, own_hits, *held_terms, [residual])
            ready = [residual]
        terms = couple(info, coupling, sources, ready)
        other_terms = exchange(terms, "crow", 1)
        held_terms = (terms, other_terms)
        if sweep_index == ITERS - 1:
            return total, add_inflow(residual, own_hits, terms, other_terms)
        steps, last = [], terms
        for s in range(subs):
            steps.append(local_solve_inflow(s, inverse_split, folds, whole, terms, other_terms, [last]))
            last = steps[-1][0]
        local, residual_parts = zip(*steps)
        half = restrict(down, z_folds, residual_parts, terms, [last])
        mine = pile(spread_over_sub(half), height)
        other = exchange(mine, "crow", 1)
        last = mine


def solution(mesh):
    return jax.shard_map(
        per_device,
        mesh=mesh,
        in_specs=(
            P("sub", "crow", "ccol"),
            P("sub", "crow", None),
            P("sub", "crow", None),
            P("sub", None, "crow"),
            P(("sub", "crow"), None),
            P("sub", None, None, None),
            P("sub", None, None),
            P("sub", None, None),
            P("sub", None),
            P("sub"),
        ),
        out_specs=(P("sub", "crow", "ccol"), P("sub", "crow", "ccol")),
        check_vma=False,
    )
```

```python
import jax
import jax.numpy as jnp
from jax import lax
from jax.experimental import pallas as pl
from jax.experimental.pallas import tpu as pltpu
from jax.sharding import PartitionSpec as P

ITERS = 2
damping = 0.7
f32 = jnp.float32
bf16 = jnp.bfloat16
MIB = 2**20
COST = 1000.0
IN_VMEM = pl.BlockSpec(memory_space=pltpu.VMEM)
IN_SMEM = pl.BlockSpec(memory_space=pltpu.SMEM)
IN_HBM = pl.BlockSpec(memory_space=pltpu.HBM)


def call(kernel, name, operands, outputs, micros, scalars=0, scratch=(), limit=8, far=0, after=()):
    used = len(operands)

    def body(*refs):
        kernel(*refs[:used], *refs[used + len(after) :])

    operands = list(operands[: used - far]) + [
        pltpu.with_memory_space_constraint(x, pltpu.HBM) for x in operands[used - far :]
    ]
    return pl.pallas_call(
        body,
        in_specs=[IN_SMEM] * scalars
        + [IN_VMEM] * (used - scalars - far)
        + [IN_HBM] * far
        + [pl.BlockSpec(memory_space=pl.ANY)] * len(after),
        out_specs=[IN_SMEM if len(shape) == 1 else IN_VMEM for shape, _ in outputs],
        out_shape=[jax.ShapeDtypeStruct(shape, kind) for shape, kind in outputs],
        scratch_shapes=list(scratch),
        compiler_params=pltpu.CompilerParams(vmem_limit_bytes=limit * MIB),
        cost_estimate=pl.CostEstimate(flops=0, bytes_accessed=int(micros * COST), transcendentals=0),
        name=name,
    )(*operands, *after)


def position():
    crow = lax.axis_index("crow")
    return lax.axis_index("sub"), lax.rem(crow, 2), crow


def parts(x):
    hi = x.astype(bf16)
    return hi, (x - hi.astype(f32)).astype(bf16)


def beside(x):
    hi, lo = parts(x)
    return jnp.concatenate([hi, lo], axis=1)


def stacked(x):
    hi, lo = parts(x)
    return jnp.concatenate([hi, lo], axis=0)


def dot(a, b):
    return jnp.dot(a, b, preferred_element_type=f32)


def sides(product):
    columns = product.shape[1] // 2
    return product[:, :columns] + product[:, columns:]


def folded(product):
    rows = product.shape[0] // 2
    return sides(product[:rows] + product[rows:])


def exchange(x, axis, bit):
    size = lax.axis_size(axis)
    return lax.ppermute(x, axis, [(i, i ^ bit) for i in range(size) if (i ^ bit) < size])


def split_matrix(matrix, name, micros, after=()):
    subs, rows, order = matrix.shape
    tile = 96 if rows % 96 == 0 else rows
    tiles = rows // tile

    def kernel(m, o, held, sems):
        crow = lax.axis_index("crow")
        copies = [
            pltpu.make_async_copy(
                m.at[i // tiles, pl.ds((i % tiles) * tile, tile)], held.at[i], sems.at[i]
            )
            for i in range(subs * tiles)
        ]
        for copy in copies:
            copy.start()
        for i, copy in enumerate(copies):
            copy.wait()
            first = (i % tiles) * tile
            for q in range(order // rows):
                column = pl.multiple_of((crow ^ q) * rows, 128)
                hi, lo = parts(held[i, :, pl.ds(column, rows)])
                o[i // tiles, first : first + tile, q * rows : (q + 1) * rows] = hi
                o[i // tiles, rows + first : rows + first + tile, q * rows : (q + 1) * rows] = lo

    return call(
        kernel,
        name,
        [matrix],
        [((subs, 2 * rows, order), bf16)],
        micros,
        far=1,
        scratch=[
            pltpu.VMEM((subs * tiles, tile, order), f32),
            pltpu.SemaphoreType.DMA((subs * tiles,)),
        ],
        after=after,
    )[0]


def place_coarse(pieces, subs, modes, own_rows, after=()):
    height, rows = pieces[0].shape
    count = len(pieces)
    order = rows * count
    spans = (height - subs * modes) // own_rows

    def kernel(*refs):
        down, up, inverse = refs[count:]
        crow = lax.axis_index("crow")
        for q, ref in enumerate(refs[:count]):
            here = slice(q * rows, (q + 1) * rows)
            for s in range(subs):
                value = ref[s * modes : (s + 1) * modes]
                down[s, :, here] = stacked(value)
                up[s, here] = beside(value.T)
            for i in range(spans):
                first = subs * modes + i * own_rows
                inverse[crow ^ q, :, i * rows : (i + 1) * rows] = ref[first : first + own_rows]

    return call(
        kernel,
        "place_coarse",
        pieces,
        [
            ((subs, 2 * modes, order), bf16),
            ((subs, order, 2 * modes), bf16),
            ((count, own_rows, spans * rows), f32),
        ],
        1.2,
        after=after,
    )


def fold_targets(counts, targets, split, basis, after=()):
    slots, subs, width = targets.shape
    rows = split.shape[1] // 2
    order = split.shape[2]
    modes = basis.shape[1] // 2
    half = subs // 2

    def kernel(n, tg, m, z, own, folds, z_folds):
        at = position()
        line = lax.broadcasted_iota(jnp.int32, (order, width), 0)
        for s in range(subs):
            for k in range(0, slots, 2):
                pair = []
                for kk in (k, k + 1):
                    aim = in_xor_order(tg[kk, s : s + 1, :], rows, order // rows, at[2])
                    aim = jnp.where(kk < n[s], aim, -1)
                    pair.append((line == aim).astype(f32).astype(bf16))
                hit = jnp.concatenate(pair, axis=1)
                here = slice(k * width, (k + 2) * width)
                own[s, :, here] = hit[:rows]
                folds[s, :, here] = dot(m[s], hit).astype(bf16)

                @pl.when(at[1] == s // half)
                def _():
                    z_folds[s % half, :, here] = dot(z[s], hit).astype(bf16)

    return call(
        kernel,
        "fold_targets",
        [counts, targets, split, basis],
        [
            ((subs, rows, slots * width), bf16),
            ((subs, 2 * rows, slots * width), bf16),
            ((half, 2 * modes, slots * width), bf16),
        ],
        4.5,
        scalars=1,
        limit=8,
        after=after,
    )


def begin(neighbour, counts, reads, basis, residual, inverse):
    subs, modes, rows = basis.shape
    cases = residual.shape[2]
    half = subs // 2
    slots, _, width = reads.shape
    used = subs * slots
    listed = -(-(used + 2) // 8) * 8
    own_rows, columns = inverse.shape
    height = subs * modes + own_rows * (columns // rows)

    def kernel(n_far, l_far, rd_far, z_far, r_far, c_far, keep, give, r, packed, both, n, c, rd, sems):
        at = position()
        pairs = [(z_far.at[s], both.at[s * modes : (s + 1) * modes]) for s in range(subs)]
        pairs.append((r_far, r))
        for i in range(columns // rows):
            first = subs * modes + i * own_rows
            pairs.append((c_far.at[:, i * rows : (i + 1) * rows], both.at[first : first + own_rows]))
        small = [(n_far, n), (l_far, c), (rd_far, rd)]
        moves = [pltpu.make_async_copy(a, b, sems.at[i]) for i, (a, b) in enumerate(small + pairs)]
        for move in moves:
            move.start()
        for move in moves[:3]:
            move.wait()
        lane = lax.broadcasted_iota(jnp.int32, (1, width), 1)
        ids = jnp.zeros((1, width), jnp.int32)
        limits = jnp.zeros((1, width), jnp.int32)
        packed[...] = jnp.zeros((listed, width), f32)
        for s in range(subs):
            for k in range(slots):
                block = s * slots + k
                packed[block : block + 1] = rd[k, s : s + 1].astype(f32)
                ids = jnp.where(lane == block, n[s, k], ids)
                limits = jnp.where(lane == block, jnp.where(k < c[s], 1, 0), limits)
        packed[used : used + 1] = ids.astype(f32)
        packed[used + 1 : used + 2] = limits.astype(f32)
        for move in moves[3:]:
            move.wait()
        for i in range(half):
            for out, first in ((keep, at[1] * half), (give, (1 - at[1]) * half)):
                s = first + i
                z = both[pl.ds(pl.multiple_of(s * modes, modes), modes)]
                out[i * modes : (i + 1) * modes] = folded(dot(stacked(z), beside(r[s])))

    return call(
        kernel,
        "begin",
        [neighbour, counts, reads, basis, residual, inverse],
        [
            ((half * modes, cases), f32),
            ((half * modes, cases), f32),
            (residual.shape, f32),
            ((listed, width), f32),
            ((height, rows), f32),
        ],
        2.0,
        far=6,
        scratch=[
            pltpu.SMEM(neighbour.shape, jnp.int32),
            pltpu.SMEM(counts.shape, jnp.int32),
            pltpu.VMEM(reads.shape, jnp.int32),
            pltpu.SemaphoreType.DMA((subs + 4 + columns // rows,)),
        ],
    )


def relay(x, after):
    def kernel(a, b):
        b[...] = a[...]

    return call(kernel, "relay", [x], [(x.shape, x.dtype)], 0.3, after=after)[0]


def in_xor_order(rows_listed, rows, blocks, crow_index):
    block = jnp.zeros_like(rows_listed)
    for q in range(1, blocks):
        block = block + (rows_listed >= q * rows).astype(jnp.int32)
    return rows_listed + ((block ^ crow_index) - block) * rows


def prepare(held, subs, slots, rows, blocks, after=()):
    ways = len(held)
    width = held[0].shape[1]
    used = subs * slots
    half = used // 2
    listed = -(-(used + 2) // 8) * 8
    starts = [h.shape[0] - listed for h in held]

    def kernel(*refs):
        at = position()
        columns, info = refs[ways:]
        info[...] = jnp.full(info.shape, -1, jnp.int32)
        for d in range(ways):
            table = refs[d][starts[d] : starts[d] + listed].astype(jnp.int32)
            picked = jnp.where(at[1] == 0, table[:half], table[half:used])
            aims = in_xor_order(picked, rows, blocks, at[2])
            spans = lax.div(aims, width)
            within = (aims - spans * width).astype(f32)
            spans = spans.astype(f32)
            for k in range(half):
                for i, line in enumerate((within, spans)):
                    tall = jnp.broadcast_to(line[k : k + 1], (width, width)).T
                    columns[d, k, i] = tall.astype(bf16)
            ids, limits = table[used : used + 1], table[used + 1 : used + 2]
            place = ids - at[0] * subs
            use = (limits > 0) & (place >= 0) & (place < subs)
            info[d : d + 1] = jnp.where(use, place, -1)
        table = refs[0][starts[0] : starts[0] + listed].astype(jnp.int32)
        ids, limits = table[used : used + 1], table[used + 1 : used + 2]
        twin = at[0] ^ 1
        inside = (ids >= at[0] * subs) & (ids < (at[0] + 1) * subs)
        paired = (ids >= twin * subs) & (ids < (twin + 1) * subs)
        theirs = jnp.where(inside, 0, jnp.where(paired, 1, 2))
        info[ways : ways + 1] = jnp.where(limits > 0, theirs, -1)

    return call(
        kernel,
        "prepare",
        list(held),
        [((ways, half, 2, width, width), bf16), ((8, width), jnp.int32)],
        0.5,
        after=after,
    )


def add_up(a, b, below=None, after=()):
    rows = a.shape[0]
    more = 0 if below is None else below.shape[0]

    def kernel(x, y, *refs):
        o = refs[-1]
        o[:rows] = x[...] + y[...]
        if more:
            o[rows:] = refs[0][...]

    operands = [a, b] + ([] if below is None else [below])
    return call(kernel, "add_up", operands, [((rows + more, a.shape[1]), f32)], 0.2, after=after)[0]


def pile(arrays, rows, after=()):
    count = len(arrays)

    def kernel(*refs):
        for i, ref in enumerate(refs[:count]):
            refs[count][i] = ref[:rows]

    columns = arrays[0].shape[1]
    return call(kernel, "pile", arrays, [((count, rows, columns), f32)], 0.2, after=after)[0]


def load(ref, s):
    return ref[s] if len(ref.shape) == 3 else ref[...]


def local_solve(s, split, blocks, after=()):
    rows = split.shape[1] // 2
    order = split.shape[2]
    cases = blocks[0].shape[-1]

    def kernel(m, *refs):
        o, rhs = refs[-2:]
        for q, ref in enumerate(refs[:-2]):
            rhs[q * rows : (q + 1) * rows] = beside(load(ref, s))
        o[...] = folded(dot(m[s], rhs[...]))

    return call(
        kernel,
        "local_solve",
        [split, *blocks],
        [((rows, cases), f32)],
        0.8,
        scratch=[pltpu.VMEM((order, 2 * cases), bf16)],
        after=after,
    )[0]


def choose_terms(here, mine, other, terms):
    slots, width = mine.shape[:2]

    @pl.when(here)
    def _():
        for k in range(slots):
            terms[k * width : (k + 1) * width] = beside(mine[k])

    @pl.when(jnp.logical_not(here))
    def _():
        for k in range(slots):
            terms[k * width : (k + 1) * width] = beside(other[k])


def local_solve_inflow(s, split, folds, blocks, mine, other, after=()):
    rows = split.shape[1] // 2
    order = split.shape[2]
    subs = split.shape[0]
    cases = blocks[0].shape[-1]
    slots, width = mine.shape[:2]
    count = len(blocks)

    def kernel(m, f, g_mine, g_other, *refs):
        at = position()
        o, rhs, terms = refs[count:]
        for q, ref in enumerate(refs[:count]):
            rhs[q * rows : (q + 1) * rows] = beside(load(ref, s))
        choose_terms(at[1] == s // (subs // 2), g_mine, g_other, terms)
        o[...] = folded(dot(m[s], rhs[...])) + damping * folded(dot(f[s], terms[...]))

    return call(
        kernel,
        "local_solve_inflow",
        [split, folds, mine, other, *blocks],
        [((rows, cases), f32), ((order, 2 * cases), bf16)],
        1.2,
        scratch=[pltpu.VMEM((slots * width, 2 * cases), bf16)],
        after=after,
    )


def restrict(basis, z_folds, residual_parts, terms, after=()):
    subs = basis.shape[0]
    modes = basis.shape[1] // 2
    cases = residual_parts[0].shape[1] // 2
    half = subs // 2
    slots, width = terms.shape[0] // half, terms.shape[1]

    def kernel(z, zf, g, *refs):
        at = position()
        out, rhs = refs[subs:]
        for i in range(half):
            for k in range(slots):
                rhs[k * width : (k + 1) * width] = beside(g[i * slots + k])
            inflow = damping * folded(dot(zf[i], rhs[...]))
            for s in range(i, subs, half):

                @pl.when(at[1] == s // half)
                def _():
                    out[i * modes : (i + 1) * modes] = folded(dot(z[s], refs[s][...])) + inflow

    return call(
        kernel,
        "restrict",
        [basis, z_folds, terms, *residual_parts],
        [((half * modes, cases), f32)],
        0.4,
        scratch=[pltpu.VMEM((slots * width, 2 * cases), bf16)],
        after=after,
    )[0]


def lift_coarse(inverse, lift, mine, other, after=()):
    subs, order, twice = lift.shape
    modes = twice // 2
    groups, _, cases = mine.shape
    half = subs // 2
    per_sub = inverse.shape[0] // subs
    columns = inverse.shape[2]

    def kernel(c, z, g_mine, g_other, o, right):
        at = position()
        for b in range(groups):
            base = (at[0] ^ b) * (2 * half * modes)
            for h, ref in ((at[1], g_mine), (1 - at[1], g_other)):
                row = pl.multiple_of(base + h * (half * modes), 16)
                right[pl.ds(row, half * modes)] = beside(ref[b])
        for s in range(subs):
            c_rows = c[s * per_sub : (s + 1) * per_sub].reshape(modes, columns)
            coarse = beside(folded(dot(stacked(c_rows), right[...])))
            o[s] = sides(dot(z[s], jnp.concatenate([coarse, coarse], axis=0)))

    return call(
        kernel,
        "lift_coarse",
        [inverse, lift, mine, other],
        [((subs, order, cases), f32)],
        1.2,
        scratch=[pltpu.VMEM((columns, 2 * cases), bf16)],
        limit=16,
        after=after,
    )[0]


def correct(lifted, blocks, info, lists, after=()):
    subs = len(blocks)
    count = len(blocks[0])
    rows, cases = blocks[0][0].shape
    order = rows * count
    ways, slots, _, width, _ = lists.shape

    def kernel(up, facts, l, *refs):
        block_refs = refs[: subs * count]
        refs = refs[subs * count :]
        corrs, outs = refs[:subs], refs[subs : subs + ways]
        where, sem = refs[subs + ways :]
        move = pltpu.make_async_copy(facts, where, sem)
        move.start()
        core = position()[1]
        for s in range(subs):
            for q in range(count):
                here = slice(q * rows, (q + 1) * rows)
                value = block_refs[s * count + q][...] + up[s, here]
                corrs[s][here] = beside(value)
        move.wait()
        lane = lax.broadcasted_iota(jnp.int32, (width, width), 1).astype(f32).astype(bf16)
        none = jnp.zeros((width, width), bf16)
        for d in range(ways):

            @pl.loop(0, slots)
            def _(k):
                place = where[d, core * slots + k]

                @pl.when(place < 0)
                def _():
                    outs[d][k] = jnp.zeros((width, cases), f32)

                for s in range(subs):

                    @pl.when(place == s)
                    def _():
                        one = jnp.where(l[d, k, 0] == lane, jnp.ones_like(none), none)
                        span = l[d, k, 1]
                        ones = [jnp.where(span == t, one, none) for t in range(order // width)]
                        outs[d][k] = sides(dot(jnp.concatenate(ones, axis=1), corrs[s][...]))

    flat = [b for of_sub in blocks for b in of_sub]
    return call(
        kernel,
        "correct",
        [lifted, info, lists, *flat],
        [((order, 2 * cases), bf16)] * subs
        + [((slots, width, cases), f32)] * ways,
        3.0,
        scratch=[pltpu.SMEM(info.shape, jnp.int32), pltpu.SemaphoreType.DMA(())],
        after=after,
    )


def reduce_residual(split, corrs, residual, lifted, own, old=None, after=()):
    subs, rows, cases = residual.shape

    def kernel(m, res, up, *refs):
        o, total = refs[-2:]
        for s in range(subs):
            o[s] = res[s] - damping * folded(dot(m[s], refs[s][...]))
            value = damping * (refs[subs + s][...] + up[s, :rows])
            total[s] = value if old is None else refs[2 * subs][s] + value

    return call(
        kernel,
        "reduce_residual",
        [split, residual, lifted, *corrs, *own] + ([] if old is None else [old]),
        [(residual.shape, f32), (residual.shape, f32)],
        1.2,
        after=after,
    )


def couple(info, coupling, sources, after=()):
    subs, per_sub, width, _ = coupling.shape
    slots, _, cases = sources[0].shape
    ways = len(sources)

    def kernel(facts, c, *refs):
        out, left, right, where, sem = refs[ways:]
        move = pltpu.make_async_copy(facts, where, sem)
        move.start()
        first = position()[1] * slots
        for k in range(slots):
            block = first + k
            left[k] = stacked(c[block // per_sub, lax.rem(block, per_sub)])
        move.wait()
        for k in range(slots):
            code = where[ways, first + k]

            @pl.when(code < 0)
            def _():
                right[k] = jnp.zeros((width, 2 * cases), bf16)

            for d, ref in enumerate(refs[:ways]):

                @pl.when(code == d)
                def _():
                    right[k] = beside(ref[k])

        for k in range(slots):
            out[k] = folded(dot(left[k], right[k]))

    return call(
        kernel,
        "couple",
        [info, coupling, *sources],
        [((slots, width, cases), f32)],
        0.8,
        scratch=[
            pltpu.VMEM((slots, 2 * width, width), bf16),
            pltpu.VMEM((slots, width, 2 * cases), bf16),
            pltpu.SMEM(info.shape, jnp.int32),
            pltpu.SemaphoreType.DMA(()),
        ],
        after=after,
    )[0]


def add_own_half(residual, hits, terms, old=None, after=()):
    subs, rows, cases = residual.shape
    slots, width, _ = terms.shape
    half = subs // 2
    per_sub = slots // half

    def kernel(res, tg, g, *refs):
        out, rhs = refs[-2:]
        core = position()[1]
        side = core if old is None else 1 - core
        for i in range(half):
            for k in range(per_sub):
                rhs[k * width : (k + 1) * width] = beside(g[i * per_sub + k])
            s = side * half + i
            value = res[s] + damping * sides(dot(tg[s], rhs[...]))
            if old is None:
                out[i] = value
            else:
                out[s] = value
                out[core * half + i] = refs[0][i]

    return call(
        kernel,
        "add_own_half",
        [residual, hits, terms] + ([] if old is None else [old]),
        [((half if old is None else subs, rows, cases), f32)],
        0.8,
        scratch=[pltpu.VMEM((per_sub * width, 2 * cases), bf16)],
        after=after,
    )[0]


def add_inflow(residual, hits, terms, others, after=()):
    own = add_own_half(residual, hits, terms, None, after)
    return add_own_half(residual, hits, others, own)


def gathered(x, hold=()):
    bit = lax.axis_size("crow") // 2
    blocks = {0: x}
    while bit >= 1:
        news = {q | bit: exchange(b, "crow", bit) for q, b in blocks.items()}
        if bit > 1 and hold:
            news = {q: relay(b, hold) for q, b in news.items()}
        blocks.update(news)
        bit //= 2
    return [blocks[q] for q in sorted(blocks)]


def spread_over_sub(half):
    return [half] + [exchange(half, "sub", b) for b in range(1, lax.axis_size("sub"))]


def pair_routes(size):
    low = [(i, i + 1) for i in range(0, size - 1, 2)]
    high = [(i, i + 1) for i in range(1, size - 1, 2)]
    return [[p for a, b in pairs for p in ((a, b), (b, a))] for pairs in (low, high)]


def per_device(
    load_cases,
    stiffness,
    local_inverse,
    coarse_basis,
    coarse_inverse,
    coupling,
    target_local_rows,
    neighbour_read_rows,
    neighbour,
    counts,
):
    subs, rows, cases = load_cases.shape
    slots = neighbour.shape[1]
    groups = lax.axis_size("sub")
    crow_size = lax.axis_size("crow")
    targets = target_local_rows.transpose(1, 0, 2)
    routes = pair_routes(groups)

    keep, give, residual, packed, both = begin(
        neighbour, counts, neighbour_read_rows.transpose(1, 0, 2), coarse_basis, load_cases,
        coarse_inverse,
    )
    keep = add_up(keep, exchange(give, "crow", 1))
    inverse_split = split_matrix(local_inverse, "split_inverse", 2.0, [keep])
    bits = [bit for bit in (2, 4, 8) if bit < crow_size]
    for bit in bits[:-1]:
        keep = add_up(keep, exchange(keep, "crow", bit), None, [inverse_split])
    more = relay(exchange(keep, "crow", bits[-1]), [inverse_split])
    first_blocks = gathered(load_cases, [more])
    both = relay(both, [more])
    local = []
    for s in range(subs):
        local.append(local_solve(s, inverse_split, first_blocks, local[-1:]))
    stiffness_split = split_matrix(stiffness, "split_stiffness", 9000.0, [local[-1]])
    local_blocks = [gathered(v, [stiffness_split]) for v in local]
    arrived = [b[crow_size // 2] for b in local_blocks]

    halves = spread_over_sub(add_up(keep, more, packed, [local[-1]]))
    height = give.shape[0]
    mine = pile(halves, height, arrived)
    other = exchange(mine, "crow", 1)
    pieces = gathered(both, [mine])
    if groups == 4:
        held = [packed, halves[1], halves[3]]
    else:
        held = [packed] + [lax.ppermute(packed, "sub", route) for route in routes]
    lists, info = prepare(held, subs, slots, rows, crow_size, [mine])
    down, lift, inverse = place_coarse(
        pieces, subs, coarse_basis.shape[1], coarse_inverse.shape[0], [info]
    )

    total, last = None, down
    for sweep_index in range(ITERS):
        if sweep_index:
            local_blocks = [gathered(v) for v in local]
        lifted = lift_coarse(inverse, lift, mine, other, [last])
        rest = correct(lifted, local_blocks, info, lists)
        corrs, chosen = rest[:subs], rest[subs:]
        sources = [chosen[0]] + [lax.ppermute(c, "sub", route) for c, route in zip(chosen[1:], routes)]
        own = [blocks[0] for blocks in local_blocks]
        residual, total = reduce_residual(stiffness_split, corrs, residual, lifted, own, total)
        if sweep_index == 0:
            own_hits, folds, z_folds = fold_targets(
                counts, targets, inverse_split, down, [residual]
            )
            whole = gathered(residual, [folds])
            ready = [folds]
        else:
            residual = add_inflow(residual, own_hits, *held_terms, [residual])
            ready = [residual]
        terms = couple(info, coupling, sources, ready)
        other_terms = exchange(terms, "crow", 1)
        held_terms = (terms, other_terms)
        if sweep_index == ITERS - 1:
            return total, add_inflow(residual, own_hits, terms, other_terms)
        steps, last = [], terms
        for s in range(subs):
            steps.append(local_solve_inflow(s, inverse_split, folds, whole, terms, other_terms, [last]))
            last = steps[-1][0]
        local, residual_parts = zip(*steps)
        half = restrict(down, z_folds, residual_parts, terms, [last])
        mine = pile(spread_over_sub(half), height)
        other = exchange(mine, "crow", 1)
        last = mine


def solution(mesh):
    return jax.shard_map(
        per_device,
        mesh=mesh,
        in_specs=(
            P("sub", "crow", "ccol"),
            P("sub", "crow", None),
            P("sub", "crow", None),
            P("sub", None, "crow"),
            P(("sub", "crow"), None),
            P("sub", None, None, None),
            P("sub", None, None),
            P("sub", None, None),
            P("sub", None),
            P("sub"),
        ),
        out_specs=(P("sub", "crow", "ccol"), P("sub", "crow", "ccol")),
        check_vma=False,
    )
```
